128 devices in a mesh: stream: 16 (over z, y), span: 2 (over core), vert: 4 (over x).
Axes of the slice: x: 4, y: 4, z: 4, core: 2. Of those that a mesh axis runs over, the one named last changes fastest.
Arguments:
- velocity: float32 [3, 48, 32, 32, 2048], P(None, None, 'vert', 'span', 'stream'), may hold values from -60 to 60, as said below
Outputs:
- modes: float32 [3, 48, 32, 32, 2048], P(None, None, 'vert', 'span', 'stream')
- factor: float32 [48, 48], replicated
The draws below stay inside these ranges and needn't reach their ends.
Inputs may be any that keep to these rules, and one draw needn't show every extreme that they name: Finite velocity components.
All inputs are finite; a program needn't handle non-finite values.
Results may differ from the reference program's by a relative error of at most 0.0003.
Values sent between devices are 32-bit elements; how exact they have to be, the bound alone decides.
No kernel may reach another device: no remote copies, remote signals or barrier semaphores. Data moves between devices by JAX's collectives and lax.ppermute only.
A program may use at most 192 MiB of HBM per device.

```python
import math
import jax
import jax.numpy as jnp
from jax import lax

SNAPS = 48
NX = 2048
NY = 32
NZ = 32
ROWS = 6291456


coherent_count = 6


def draw_velocity(key, part):
    subkeys = jax.random.split(key, 7)
    shape_all = (3, SNAPS, NZ, NY, NX)
    spread = math.log(10.0)
    floor_level = 0.25
    jitter = jax.random.truncated_normal(subkeys[0], -4.0, 4.0, shape_all, jnp.float32)
    row_scale = jnp.exp(jax.random.uniform(subkeys[1], (1, 1, NZ, NY, NX), jnp.float32) * spread)
    position = jnp.arange(NX, dtype=jnp.float32) / max(NX - 1, 1)
    downstream = jnp.exp(position * math.log(3.0))
    column_scale = jnp.exp(jax.random.uniform(subkeys[2], (1, SNAPS, 1, 1, 1), jnp.float32) * math.log(4.0))
    moments = jnp.arange(SNAPS, dtype=jnp.float32)
    angular = jax.random.uniform(subkeys[3], (coherent_count,), jnp.float32, 0.1, 0.6)
    phases = jax.random.uniform(subkeys[4], (coherent_count,), jnp.float32, -math.pi, math.pi)
    growth = jax.random.uniform(subkeys[5], (coherent_count,), jnp.float32, -1.0, 0.5)
    mode_keys = jax.random.split(subkeys[6], coherent_count)
    coherent = floor_level * jitter
    for number in range(coherent_count):
        pattern = jax.random.truncated_normal(mode_keys[number], -4.0, 4.0, (3, 1, NZ, NY, NX), jnp.float32)
        series = 0.5 ** number * jnp.cos(angular[number] * moments + phases[number]) * jnp.exp(growth[number] * moments / SNAPS)
        coherent = coherent + series.reshape(1, SNAPS, 1, 1, 1) * pattern
    return 0.02 * coherent * row_scale * column_scale * downstream


def setup_inputs(seed: int = 0) -> dict:
    arg_keys = jax.random.split(jax.random.key(seed), 2)
    velocity = draw_velocity(jax.random.fold_in(arg_keys[1], 71), 0)
    return dict(velocity=velocity)


HIGH = lax.Precision.HIGHEST

def curl_operator(padded_streamwise_velocity, padded_vertical_velocity, padded_spanwise_velocity):
    dz_u = padded_streamwise_velocity[:, 2:, 1:-1, :] - padded_streamwise_velocity[:, :-2, 1:-1, :]
    dy_u = padded_streamwise_velocity[:, 1:-1, 2:, :] - padded_streamwise_velocity[:, 1:-1, :-2, :]
    spanwise_vertical_slope = padded_vertical_velocity[:, 2:, :, 1:-1] - padded_vertical_velocity[:, :-2, :, 1:-1]
    streamwise_vertical_slope = padded_vertical_velocity[:, 1:-1, :, 2:] - padded_vertical_velocity[:, 1:-1, :, :-2]
    dy_w = padded_spanwise_velocity[:, :, 2:, 1:-1] - padded_spanwise_velocity[:, :, :-2, 1:-1]
    dx_w = padded_spanwise_velocity[:, :, 1:-1, 2:] - padded_spanwise_velocity[:, :, 1:-1, :-2]
    return jnp.stack([0.5 * (dy_w - spanwise_vertical_slope), 0.5 * (dz_u - dx_w), 0.5 * (streamwise_vertical_slope - dy_u)])

def gram(field):
    return jnp.einsum('cszyx,ctzyx->st', field, field, precision=HIGH)

def apply_left(matrix, field):
    return jnp.einsum('st,ctzyx->cszyx', matrix, field, precision=HIGH)

def lower_inverse(gram_matrix):
    lower = jnp.linalg.cholesky(gram_matrix)
    ident = jnp.eye(gram_matrix.shape[0], dtype=jnp.float32)
    return (lower, lax.linalg.triangular_solve(lower, ident, left_side=True, lower=True))

def reference(velocity):
    padded_streamwise_velocity = jnp.pad(velocity[0], ((0, 0), (1, 1), (1, 1), (0, 0)))
    padded_vertical_velocity = jnp.pad(velocity[1], ((0, 0), (1, 1), (0, 0), (1, 1)))
    padded_spanwise_velocity = jnp.pad(velocity[2], ((0, 0), (0, 0), (1, 1), (1, 1)))
    vorticity_field = curl_operator(padded_streamwise_velocity, padded_vertical_velocity, padded_spanwise_velocity)
    count = float(ROWS)
    lower, inverse = lower_inverse(gram(vorticity_field) / count)
    modes = apply_left(inverse, vorticity_field)
    factor = lower.T
    return (modes, factor)
```

```python
import functools

import jax
import jax.numpy as jnp
from jax import lax
from jax.experimental import pallas as pl
from jax.experimental.pallas import tpu as pltpu
from jax.sharding import PartitionSpec as P

F32, BF16 = jnp.float32, jnp.bfloat16
HIGH = lax.Precision.HIGHEST
S, NZ, NY, NX = 48, 8, 16, 128
ROWS = NZ * NY
SUB = 8
R = S * SUB
PAIR = 2 * NX
INTERIOR = 20 * PAIR
COLS = 24 * PAIR
MIB = 1 << 20
ALL = ("stream", "span", "vert")
NT = (((1,), (1,)), ((), ()))


def slot(c, z):
    if c == 2:
        return 12 + z
    return c * 6 + z - 1 if 0 < z < NZ - 1 else 20 + 2 * c + (z == NZ - 1)


def any_spec():
    return pl.BlockSpec(memory_space=pl.ANY)


def vmem_spec():
    return pl.BlockSpec(memory_space=pltpu.VMEM)


def params(limit):
    return pltpu.CompilerParams(vmem_limit_bytes=limit * MIB)


def in_vmem(*arrays):
    return [pltpu.with_memory_space_constraint(a, pltpu.VMEM) for a in arrays]


def vertical_faces_kernel(v_ref, head_ref, tail_ref, sems):
    low = pltpu.make_async_copy(v_ref.at[0:2, :, pl.ds(0, NY)], head_ref, sems.at[0])
    high = pltpu.make_async_copy(v_ref.at[0:2, :, pl.ds(ROWS - NY, NY)], tail_ref, sems.at[1])
    low.start()
    high.start()
    low.wait()
    high.wait()


def vertical_faces(v):
    face = pltpu.VMEM((2, S, NY, NX), F32)
    return pl.pallas_call(
        vertical_faces_kernel,
        name="vertical_faces",
        out_shape=(face, face),
        in_specs=[any_spec()],
        out_specs=(vmem_spec(), vmem_spec()),
        scratch_shapes=[pltpu.SemaphoreType.DMA((2,))],
        compiler_params=params(8),
    )(v)


def side_faces_kernel(v_ref, block_ref, x_ref, y_ref, sems):
    copies = [pltpu.make_async_copy(v_ref.at[c], block_ref.at[c], sems.at[c]) for c in range(3)]
    for c in (1, 2, 0):
        copies[c].start()
    lane = lax.broadcasted_iota(jnp.int32, (NY, NX), 1) // 2
    for c in (1, 2):
        copies[c].wait()

        def pack(z, carry, c=c):
            rows = pl.ds(pl.multiple_of(z * NY, NY), NY)
            packed = jnp.zeros((NY, NX), F32)
            for s in range(S):
                turned = pltpu.roll(block_ref[c, s, rows, :], 2 * s + 1, axis=1)
                packed = jnp.where(lane == s, turned, packed)
            x_ref[c - 1, rows, :] = packed
            return carry

        lax.fori_loop(0, NZ, pack, 0)
    copies[0].wait()
    first = lax.axis_index("span") == 0
    for k, c in enumerate((0, 2)):
        for s in range(S):
            high = block_ref[c, s, pl.ds(NY - 1, NZ, stride=NY), :]
            low = block_ref[c, s, pl.ds(0, NZ, stride=NY), :]
            y_ref[k, s] = jnp.where(first, high, low)


def side_faces(v):
    return pl.pallas_call(
        side_faces_kernel,
        name="side_faces",
        out_shape=(
            pltpu.VMEM((3, S, ROWS, NX), F32),
            pltpu.VMEM((2, ROWS, NX), F32),
            pltpu.VMEM((2, S, NZ, NX), F32),
        ),
        in_specs=[any_spec()],
        out_specs=(vmem_spec(), vmem_spec(), vmem_spec()),
        scratch_shapes=[pltpu.SemaphoreType.DMA((3,))],
        compiler_params=params(16),
    )(v)


def split_store(first, second, pair, columns, h_ref, l_ref):
    for half in range(2):
        rows = slice(half * SUB, (half + 1) * SUB)
        value = jnp.concatenate([first[rows], second[rows]], axis=0)
        high = value.astype(BF16)
        low = ((value - high.astype(F32)) * 2.0).astype(BF16)
        where = (pl.ds(pair * 2 * SUB, 2 * SUB), pl.ds(pl.multiple_of(columns + half * NX, NX), NX))
        h_ref[where] = high
        l_ref[where] = low


def interior_kernel(v_ref, hy_ref, left_ref, right_ref, h_ref, l_ref, part_ref, acc_ref, edge_ref):
    row = lax.broadcasted_iota(jnp.int32, (NY, NX), 0)
    lane = lax.broadcasted_iota(jnp.int32, (NY, NX), 1)
    span, stream = lax.axis_index("span"), lax.axis_index("stream")
    first = span == 0
    for c in range(2):
        for z in range(NZ):
            rows = pl.ds(z * NY, NY)
            before = jnp.where(stream > 0, left_ref[c, rows, :], 0.0)
            behind = jnp.where(stream < lax.axis_size("stream") - 1, right_ref[c, rows, :], 0.0)
            edge_ref[c, rows, :] = jnp.where(lane % 2 == 0, before, pltpu.roll(behind, NX - 2, axis=1))

    def at(z):
        return pl.ds(pl.multiple_of(z * NY, NY), NY)

    def dy(c, s, z):
        cells = v_ref[c, s, at(z), :]
        face = hy_ref[c // 2, s, pl.ds(z, 1), :]
        up = jnp.where(row == NY - 1, jnp.where(first, face, 0.0), pltpu.roll(cells, NY - 1, axis=0))
        down = jnp.where(row == 0, jnp.where(first, 0.0, face), pltpu.roll(cells, 1, axis=0))
        return up - down

    def dx(c, s, z):
        cells = v_ref[c, s, at(z), :]
        edge = edge_ref[c - 1, at(z), :]
        if s:
            edge = pltpu.roll(edge, NX - 2 * s, axis=1)
        up = jnp.where(lane == NX - 1, edge, pltpu.roll(cells, NX - 1, axis=1))
        down = jnp.where(lane == 0, edge, pltpu.roll(cells, 1, axis=1))
        return up - down

    def dz(c, s, z):
        return v_ref[c, s, at(z + 1), :] - v_ref[c, s, at(z - 1), :]

    def inner(z, carry):
        for s in range(0, S, 2):
            split_store(
                *(0.5 * (dy(2, t, z) - dz(1, t, z)) for t in (s, s + 1)),
                s // 2, (z - 1) * PAIR, h_ref, l_ref,
            )
            split_store(
                *(0.5 * (dz(0, t, z) - dx(2, t, z)) for t in (s, s + 1)),
                s // 2, (z + 5) * PAIR, h_ref, l_ref,
            )
        return carry

    def level(z, carry):
        for s in range(0, S, 2):
            split_store(
                *(0.5 * (dx(1, t, z) - dy(0, t, z)) for t in (s, s + 1)),
                s // 2, (z + 12) * PAIR, h_ref, l_ref,
            )
        return carry

    def outer(k, carry):
        z = k * (NZ - 1)
        for s in range(S):
            part_ref[0, k, s] = dy(2, s, z)
            part_ref[1, k, s] = dx(2, s, z)
        return carry

    lax.fori_loop(1, NZ - 1, inner, 0)
    lax.fori_loop(0, NZ, level, 0)
    lax.fori_loop(0, 2, outer, 0)

    acc_ref[...] = jnp.zeros_like(acc_ref)
    step = 4 * PAIR

    def products(k, carry):
        columns = pl.ds(pl.multiple_of(k * step, step), step)
        high = h_ref[:, columns]
        acc_ref[...] += lax.dot_general(high, high, NT, preferred_element_type=F32) + lax.dot_general(
            high, l_ref[:, columns], NT, preferred_element_type=F32
        )
        return carry

    lax.fori_loop(0, INTERIOR // step, products, 0)


def interior(block, hy, left, right):
    return pl.pallas_call(
        interior_kernel,
        name="interior",
        out_shape=(
            pltpu.VMEM((R, COLS), BF16),
            pltpu.VMEM((R, COLS), BF16),
            pltpu.VMEM((2, 2, S, NY, NX), F32),
            pltpu.VMEM((R, R), F32),
        ),
        in_specs=[vmem_spec()] * 4,
        out_specs=(vmem_spec(),) * 4,
        scratch_shapes=[pltpu.VMEM((2, ROWS, NX), F32)],
        compiler_params=params(16),
        cost_estimate=pl.CostEstimate(flops=4 * R * R * INTERIOR, bytes_accessed=30 * MIB, transcendentals=0),
    )(*in_vmem(block, hy, left, right))


def lane_fold():
    shape = (R, NX)
    same = lax.broadcasted_iota(jnp.int32, shape, 0) // SUB == lax.broadcasted_iota(jnp.int32, shape, 1)
    return jnp.where(same, 1.0, 0.0)


def same_cell():
    return lax.broadcasted_iota(jnp.int32, (R, R), 0) % SUB == lax.broadcasted_iota(jnp.int32, (R, R), 1) % SUB


def boundary_kernel(v_ref, part_ref, below_ref, above_ref, acc_ref, hi_ref, li_ref, h_ref, l_ref, gram_ref):
    del hi_ref, li_ref
    vert = lax.axis_index("vert")
    has_below, has_above = vert > 0, vert < lax.axis_size("vert") - 1

    def dz(c, s, k):
        if k:
            return jnp.where(has_above, above_ref[c, s], 0.0) - v_ref[c, s, pl.ds((NZ - 2) * NY, NY), :]
        return v_ref[c, s, pl.ds(NY, NY), :] - jnp.where(has_below, below_ref[c, s], 0.0)

    for k in range(2):
        for s in range(0, S, 2):
            split_store(
                *(0.5 * (part_ref[0, k, t] - dz(1, t, k)) for t in (s, s + 1)),
                s // 2, (20 + k) * PAIR, h_ref, l_ref,
            )
            split_store(
                *(0.5 * (dz(0, t, k) - part_ref[1, k, t]) for t in (s, s + 1)),
                s // 2, (22 + k) * PAIR, h_ref, l_ref,
            )
    columns = pl.ds(INTERIOR, COLS - INTERIOR)
    high = h_ref[:, columns]
    total = (
        acc_ref[...]
        + lax.dot_general(high, high, NT, preferred_element_type=F32)
        + lax.dot_general(high, l_ref[:, columns], NT, preferred_element_type=F32)
    )
    total = jnp.where(same_cell(), total, 0.0).reshape(S, SUB, R).sum(1)
    gram_ref[...] = lax.dot_general(
        total, lane_fold(), (((1,), (0,)), ((), ())), precision=HIGH, preferred_element_type=F32
    )


def boundary(block, part, below, above, acc, high, low):
    return pl.pallas_call(
        boundary_kernel,
        name="boundary",
        out_shape=(
            pltpu.VMEM((R, COLS), BF16),
            pltpu.VMEM((R, COLS), BF16),
            pltpu.VMEM((S, NX), F32),
        ),
        in_specs=[vmem_spec()] * 5 + [any_spec()] * 2,
        out_specs=(vmem_spec(),) * 3,
        input_output_aliases={5: 0, 6: 1},
        compiler_params=params(16),
    )(*in_vmem(block, part, below, above, acc, high, low))


def modes_kernel(count, gram_ref, h_ref, l_ref, out_ref, factor_ref, wh_ref, wl_ref):
    @pl.when((pl.program_id(0) == 0) & (pl.program_id(1) == 0))
    def _():
        shape = (S, NX)
        row = lax.broadcasted_iota(jnp.int32, shape, 0)
        lane = lax.broadcasted_iota(jnp.int32, shape, 1)
        raw = gram_ref[...] / count
        square = jnp.concatenate([raw, jnp.zeros((NX - S, NX), F32)], axis=0)
        work = 0.5 * (raw + square.T[:S]) + jnp.where(lane == row + NX // 2, 1.0, 0.0)
        for k in range(S - 1):
            pivot = work[k : k + 1, :]
            scaled = pivot / pivot[:, k : k + 1]
            work = work - jnp.where(row > k, work[:, k : k + 1], 0.0) * scaled
        diagonal = jnp.sum(jnp.where(lane == row, work, 0.0), axis=1, keepdims=True)
        work = work * lax.rsqrt(diagonal)
        factor_ref[...] = jnp.where(lane >= row, work, 0.0)[:, :S]
        inverse = jnp.where(lane <= row, pltpu.roll(work, NX // 2, axis=1), 0.0)
        high = inverse.astype(BF16).astype(F32)
        both = jnp.concatenate([high, inverse - high], axis=0).astype(BF16)
        wide = lax.dot_general(both, lane_fold().astype(BF16), NT, preferred_element_type=F32)
        same = same_cell()
        for part, ref in ((wide[:S], wh_ref), (wide[S:], wl_ref)):
            tall = jnp.broadcast_to(part[:, None, :], (S, SUB, R)).reshape(R, R)
            ref[...] = jnp.where(same, tall, 0.0).astype(BF16)

    c = pl.program_id(0)
    levels = out_ref.shape[2]
    cut = 2 * PAIR // 2
    for k in range(levels):
        z = pl.program_id(1) * levels + k
        edge = 20 + 2 * c + jnp.where(z == NZ - 1, 1, 0)
        place = jnp.where(c == 2, 12 + z, jnp.where((z == 0) | (z == NZ - 1), edge, c * 6 + z - 1))
        columns = pl.ds(pl.multiple_of(place * PAIR, PAIR), PAIR)
        for low, up, depth in ((0, cut, cut), (cut, R, R)):
            wh, wl = wh_ref[low:up, :depth], wl_ref[low:up, :depth]
            h, l = h_ref[:depth, columns], l_ref[:depth, columns]
            part = (
                jnp.dot(wh, h, preferred_element_type=F32)
                + jnp.dot(wl, h, preferred_element_type=F32)
                + jnp.dot(wh * jnp.asarray(0.5, BF16), l, preferred_element_type=F32)
            )
            for half in range(2):
                tile = part[:, half * NX : (half + 1) * NX].reshape((up - low) // SUB, SUB, NX)
                out_ref[0, low // SUB : up // SUB, k, half * SUB : (half + 1) * SUB, :] = tile


def modes_and_factor(gram, high, low, count):
    levels = 2
    gram, high, low = in_vmem(gram, high, low)
    return pl.pallas_call(
        functools.partial(modes_kernel, count),
        name="modes",
        grid=(3, NZ // levels),
        out_shape=(
            jax.ShapeDtypeStruct((3, S, NZ, NY, NX), F32),
            jax.ShapeDtypeStruct((S, S), F32),
        ),
        in_specs=[vmem_spec()] * 3,
        out_specs=(
            pl.BlockSpec((1, S, levels, NY, NX), lambda c, z: (c, 0, z, 0, 0)),
            pl.BlockSpec((S, S), lambda c, z: (0, 0)),
        ),
        scratch_shapes=[pltpu.VMEM((R, R), BF16), pltpu.VMEM((R, R), BF16)],
        compiler_params=params(24),
    )(gram, high, low)


def ring(axis, shift):
    count = lax.axis_size(axis)
    return [(i, (i + shift) % count) for i in range(count)]


def total_over_devices(gram):
    gram = gram + lax.ppermute(gram, "span", ring("span", 1))
    gram = gram + lax.ppermute(gram, "vert", [(i, i ^ 1) for i in range(4)])
    gram = gram + lax.ppermute(gram, "vert", [(i, i ^ 3) for i in range(4)])
    for flip in (1, 3, 4, 12):
        gram = gram + lax.ppermute(gram, "stream", [(i, i ^ flip) for i in range(16)])
    return gram


def per_device(velocity):
    v = velocity.reshape(3, S, ROWS, NX)
    head, tail = vertical_faces(v)
    below = lax.ppermute(tail, "vert", ring("vert", 1))
    above = lax.ppermute(head, "vert", ring("vert", -1))
    block, xs, ys = side_faces(v)
    hy = lax.ppermute(ys, "span", ring("span", 1))
    left = lax.ppermute(xs, "stream", ring("stream", 1))
    right = lax.ppermute(xs, "stream", ring("stream", -1))
    high, low, part, acc = interior(block, hy, left, right)
    high, low, gram = boundary(block, part, below, above, acc, high, low)
    gram = total_over_devices(gram)
    devices = lax.axis_size("stream") * lax.axis_size("span") * lax.axis_size("vert")
    count = float(3 * NZ * NY * NX * devices)
    return modes_and_factor(gram, high, low, count)


def solution(mesh):
    spec = P(None, None, "vert", "span", "stream")
    return jax.shard_map(per_device, mesh=mesh, in_specs=(spec,), out_specs=(spec, P()), check_vma=False)
```

```python
import functools

import jax
import jax.numpy as jnp
from jax import lax
from jax.experimental import pallas as pl
from jax.experimental.pallas import tpu as pltpu
from jax.sharding import PartitionSpec as P

F32, BF16 = jnp.float32, jnp.bfloat16
HIGH = lax.Precision.HIGHEST
S, NZ, NY, NX = 48, 8, 16, 128
ROWS = NZ * NY
SUB = 8
R = S * SUB
PAIR = 2 * NX
MIB = 1 << 20
NT = (((1,), (1,)), ((), ()))


def any_spec():
    return pl.BlockSpec(memory_space=pl.ANY)


def vmem_spec():
    return pl.BlockSpec(memory_space=pltpu.VMEM)


def params(limit):
    return pltpu.CompilerParams(vmem_limit_bytes=limit * MIB)


def in_vmem(*arrays):
    return [pltpu.with_memory_space_constraint(a, pltpu.VMEM) for a in arrays]


def in_hbm(array):
    return pltpu.with_memory_space_constraint(array, pltpu.HBM)


def vertical_faces_kernel(v_ref, head_ref, tail_ref, sems):
    low = pltpu.make_async_copy(v_ref.at[0:2, :, pl.ds(0, NY)], head_ref, sems.at[0])
    high = pltpu.make_async_copy(v_ref.at[0:2, :, pl.ds(ROWS - NY, NY)], tail_ref, sems.at[1])
    low.start()
    high.start()
    low.wait()
    high.wait()


def vertical_faces(v):
    face = pltpu.VMEM((2, S, NY, NX), F32)
    return pl.pallas_call(
        vertical_faces_kernel,
        name="vertical_faces",
        out_shape=(face, face),
        in_specs=[any_spec()],
        out_specs=(vmem_spec(), vmem_spec()),
        scratch_shapes=[pltpu.SemaphoreType.DMA((2,))],
        compiler_params=params(8),
    )(in_hbm(v))


def side_faces_kernel(block_ref, x_ref, y_ref):
    lane = lax.broadcasted_iota(jnp.int32, (NY, NX), 1) // 2
    for c in (1, 2):

        def pack(z, carry, c=c):
            rows = pl.ds(pl.multiple_of(z * NY, NY), NY)
            packed = jnp.zeros((NY, NX), F32)
            for s in range(S):
                turned = pltpu.roll(block_ref[c, s, rows, :], 2 * s + 1, axis=1)
                packed = jnp.where(lane == s, turned, packed)
            x_ref[c - 1, rows, :] = packed
            return carry

        lax.fori_loop(0, NZ, pack, 0)
    first = lax.axis_index("span") == 0
    for k, c in enumerate((0, 2)):
        for s in range(S):
            high = block_ref[c, s, pl.ds(NY - 1, NZ, stride=NY), :]
            low = block_ref[c, s, pl.ds(0, NZ, stride=NY), :]
            y_ref[k, s] = jnp.where(first, high, low)


def side_faces(block):
    return pl.pallas_call(
        side_faces_kernel,
        name="side_faces",
        out_shape=(
            pltpu.VMEM((2, ROWS, NX), F32),
            pltpu.VMEM((2, S, NZ, NX), F32),
        ),
        in_specs=[vmem_spec()],
        out_specs=(vmem_spec(), vmem_spec()),
        compiler_params=params(8),
    )(*in_vmem(block))


def split_store(first, second, pair, place, h_ref, l_ref):
    for half in range(2):
        rows = slice(half * SUB, (half + 1) * SUB)
        value = jnp.concatenate([first[rows], second[rows]], axis=0)
        high = value.astype(BF16)
        low = ((value - high.astype(F32)) * 2.0).astype(BF16)
        where = (place, pl.ds(pair * 2 * SUB, 2 * SUB), pl.ds(half * NX, NX))
        h_ref[where] = high
        l_ref[where] = low


def products(h_ref, l_ref, places):
    highs, lows = [h_ref[p] for p in places], [l_ref[p] for p in places]
    left, right = jnp.concatenate(highs + highs, axis=1), jnp.concatenate(highs + lows, axis=1)
    return lax.dot_general(left, right, NT, preferred_element_type=F32)


def level(z):
    return pl.ds(pl.multiple_of(z * NY, NY), NY)


def slope_z(v_ref, c, s, z):
    return v_ref[c, s, level(z + 1), :] - v_ref[c, s, level(z - 1), :]


def slope_y(v_ref, hy_ref, c, s, z):
    row = lax.broadcasted_iota(jnp.int32, (NY, NX), 0)
    first = lax.axis_index("span") == 0
    cells = v_ref[c, s, level(z), :]
    face = hy_ref[c // 2, s, pl.ds(z, 1), :]
    up = jnp.where(row == NY - 1, jnp.where(first, face, 0.0), pltpu.roll(cells, NY - 1, axis=0))
    down = jnp.where(row == 0, jnp.where(first, 0.0, face), pltpu.roll(cells, 1, axis=0))
    return up - down


def slope_x(v_ref, edge_ref, c, s, z):
    lane = lax.broadcasted_iota(jnp.int32, (NY, NX), 1)
    cells = v_ref[c, s, level(z), :]
    edge = edge_ref[c - 1, level(z), :]
    if s:
        edge = pltpu.roll(edge, NX - 2 * s, axis=1)
    up = jnp.where(lane == NX - 1, edge, pltpu.roll(cells, NX - 1, axis=1))
    down = jnp.where(lane == 0, edge, pltpu.roll(cells, 1, axis=1))
    return up - down


def send_out(places, scratch, refs, sems):
    for i, (a, b) in enumerate(zip(scratch, refs)):
        for p in places:
            pltpu.make_async_copy(a.at[p], b.at[p], sems.at[i]).start()


def wait_out(scratch, refs, sems):
    for i, (a, b) in enumerate(zip(scratch, refs)):
        pltpu.make_async_copy(a, b, sems.at[i]).wait()


def first_kernel(v_ref, hy_ref, h_out, l_out, part_ref, acc_ref, h_ref, l_ref, sems):
    def vorticity(z):
        for s in range(0, S, 2):
            pair = (0.5 * (slope_y(v_ref, hy_ref, 2, t, z) - slope_z(v_ref, 1, t, z)) for t in (s, s + 1))
            split_store(*pair, s // 2, z - 1, h_ref, l_ref)
        send_out([z - 1], (h_ref, l_ref), (h_out, l_out), sems)

    def step(z, carry):
        acc_ref[...] += products(h_ref, l_ref, [z - 2])
        vorticity(z)
        return carry

    acc_ref[...] = jnp.zeros_like(acc_ref)
    vorticity(1)
    lax.fori_loop(2, NZ - 1, step, 0)
    acc_ref[...] += products(h_ref, l_ref, [NZ - 3])

    def outer(k, carry):
        for s in range(S):
            part_ref[k, s] = slope_y(v_ref, hy_ref, 2, s, k * (NZ - 1))
        return carry

    lax.fori_loop(0, 2, outer, 0)
    wait_out((h_ref, l_ref), (h_out, l_out), sems)


def first_component(block, hy):
    half = pltpu.HBM((6, R, PAIR), BF16)
    return pl.pallas_call(
        first_kernel,
        name="first_component",
        out_shape=(half, half, pltpu.VMEM((2, S, NY, NX), F32), pltpu.VMEM((R, R), F32)),
        in_specs=[vmem_spec()] * 2,
        out_specs=(any_spec(), any_spec(), vmem_spec(), vmem_spec()),
        scratch_shapes=[pltpu.VMEM((6, R, PAIR), BF16)] * 2 + [pltpu.SemaphoreType.DMA((2,))],
        compiler_params=params(8),
        cost_estimate=pl.CostEstimate(flops=4 * R * R * 6 * PAIR, bytes_accessed=6 * MIB, transcendentals=0),
    )(*in_vmem(block, hy))


def rest_kernel(v_ref, hy_ref, left_ref, right_ref, old_ref, h_out, l_out, part_ref, acc_ref, edge_ref, h_ref, l_ref, sems):
    lane = lax.broadcasted_iota(jnp.int32, (NY, NX), 1)
    stream = lax.axis_index("stream")
    for c in range(2):
        for z in range(NZ):
            rows = pl.ds(z * NY, NY)
            before = jnp.where(stream > 0, left_ref[c, rows, :], 0.0)
            behind = jnp.where(stream < lax.axis_size("stream") - 1, right_ref[c, rows, :], 0.0)
            edge_ref[c, rows, :] = jnp.where(lane % 2 == 0, before, pltpu.roll(behind, NX - 2, axis=1))

    def second(z):
        for s in range(0, S, 2):
            pair = (0.5 * (slope_z(v_ref, 0, t, z) - slope_x(v_ref, edge_ref, 2, t, z)) for t in (s, s + 1))
            split_store(*pair, s // 2, z - 1, h_ref, l_ref)
        send_out([z - 1], (h_ref, l_ref), (h_out, l_out), sems)

    def third(z):
        for s in range(0, S, 2):
            pair = (
                0.5 * (slope_x(v_ref, edge_ref, 1, t, z) - slope_y(v_ref, hy_ref, 0, t, z)) for t in (s, s + 1)
            )
            split_store(*pair, s // 2, z + 6, h_ref, l_ref)
        send_out([z + 6], (h_ref, l_ref), (h_out, l_out), sems)

    def step(z, carry):
        acc_ref[...] += products(h_ref, l_ref, [z - 2, z + 5])
        second(z)
        third(z)
        return carry

    third(0)
    acc_ref[...] = old_ref[...] + products(h_ref, l_ref, [6])
    second(1)
    third(1)
    lax.fori_loop(2, NZ - 1, step, 0)
    acc_ref[...] += products(h_ref, l_ref, [NZ - 3, NZ + 4])
    third(NZ - 1)
    acc_ref[...] += products(h_ref, l_ref, [NZ + 5])

    def outer(k, carry):
        for s in range(S):
            part_ref[k, s] = slope_x(v_ref, edge_ref, 2, s, k * (NZ - 1))
        return carry

    lax.fori_loop(0, 2, outer, 0)
    wait_out((h_ref, l_ref), (h_out, l_out), sems)


def other_components(block, hy, left, right, acc):
    half = pltpu.HBM((14, R, PAIR), BF16)
    return pl.pallas_call(
        rest_kernel,
        name="other_components",
        out_shape=(half, half, pltpu.VMEM((2, S, NY, NX), F32), pltpu.VMEM((R, R), F32)),
        in_specs=[vmem_spec()] * 5,
        out_specs=(any_spec(), any_spec(), vmem_spec(), vmem_spec()),
        scratch_shapes=[pltpu.VMEM((2, ROWS, NX), F32)]
        + [pltpu.VMEM((14, R, PAIR), BF16)] * 2
        + [pltpu.SemaphoreType.DMA((2,))],
        compiler_params=params(12),
        cost_estimate=pl.CostEstimate(flops=4 * R * R * 14 * PAIR, bytes_accessed=12 * MIB, transcendentals=0),
    )(*in_vmem(block, hy, left, right, acc))


def lane_fold():
    shape = (R, NX)
    same = lax.broadcasted_iota(jnp.int32, shape, 0) // SUB == lax.broadcasted_iota(jnp.int32, shape, 1)
    return jnp.where(same, 1.0, 0.0)


def same_cell():
    return lax.broadcasted_iota(jnp.int32, (R, R), 0) % SUB == lax.broadcasted_iota(jnp.int32, (R, R), 1) % SUB


def boundary_kernel(
    v_ref, wy_ref, wx_ref, below_ref, above_ref, acc_ref, h_ref, l_ref, mine_ref, other_ref
):
    vert = lax.axis_index("vert")
    has_below, has_above = vert > 0, vert < lax.axis_size("vert") - 1

    def dz(c, s, k):
        if k:
            return jnp.where(has_above, above_ref[c, s], 0.0) - v_ref[c, s, pl.ds((NZ - 2) * NY, NY), :]
        return v_ref[c, s, pl.ds(NY, NY), :] - jnp.where(has_below, below_ref[c, s], 0.0)

    for k in range(2):
        for s in range(0, S, 2):
            split_store(
                *(0.5 * (wy_ref[k, t] - dz(1, t, k)) for t in (s, s + 1)),
                s // 2, k, h_ref, l_ref,
            )
            split_store(
                *(0.5 * (dz(0, t, k) - wx_ref[k, t]) for t in (s, s + 1)),
                s // 2, 2 + k, h_ref, l_ref,
            )
    total = acc_ref[...] + products(h_ref, l_ref, range(4))
    total = jnp.where(same_cell(), total, 0.0).reshape(S, SUB, R).sum(1)
    total = lax.dot_general(
        total, lane_fold(), (((1,), (0,)), ((), ())), precision=HIGH, preferred_element_type=F32
    )
    square = jnp.concatenate([total, jnp.zeros((NX - S, NX), F32)], axis=0)
    total = 0.5 * (total + square.T[:S])
    lane = lax.broadcasted_iota(jnp.int32, (SUB, NX), 1)
    groups = [total[g * SUB : (g + 1) * SUB] for g in range(S // SUB)]
    bottom = jnp.where(lane < 48, groups[4], pltpu.roll(groups[5], 48, axis=1))
    top = jnp.where(lane < 64, pltpu.roll(groups[2], 32, axis=1), pltpu.roll(groups[3], 64, axis=1))
    top = jnp.where(lane < 16, groups[0], jnp.where(lane < 32, pltpu.roll(groups[1], 16, axis=1), top))
    first = lax.axis_index("span") == 0
    mine_ref[...] = jnp.where(first, top, bottom)
    other_ref[...] = jnp.where(first, bottom, top)


def boundary(block, wy, wx, below, above, acc):
    half = pltpu.VMEM((4, R, PAIR), BF16)
    sums = pltpu.VMEM((SUB, NX), F32)
    return pl.pallas_call(
        boundary_kernel,
        name="boundary",
        out_shape=(half, half, sums, sums),
        in_specs=[vmem_spec()] * 6,
        out_specs=(vmem_spec(),) * 4,
        compiler_params=params(8),
    )(*in_vmem(block, wy, wx, below, above, acc))


def eliminate(work):
    row = lax.broadcasted_iota(jnp.int32, (SUB, NX), 0)

    def spread(part):
        return jnp.broadcast_to(part, (SUB, NX))

    width = SUB
    for start in range(0, S, width):
        home, base = start // SUB, start % SUB
        live = range(home, S // SUB)
        pivots = [spread(work[home][base + j : base + j + 1, :]) for j in range(width)]
        cols = [{g: spread(work[g][:, start + j : start + j + 1]) for g in live} for j in range(width)]
        heads = [[spread(cols[j][home][base + i : base + i + 1, :]) for j in range(width)] for i in range(width)]
        for i in range(width):
            scale = 1.0 / heads[i][i]
            for j in range(i + 1, width):
                ratio = heads[i][j] * scale
                pivots[j] = pivots[j] - ratio * pivots[i]
                for g in live:
                    cols[j][g] = cols[j][g] - ratio * cols[i][g]
                for k in range(j, width):
                    heads[j][k] = heads[j][k] - ratio * heads[i][k]
            for g in live:
                factor = cols[i][g] * scale
                if g == home:
                    factor = jnp.where(row > base + i, factor, 0.0)
                work[g] = work[g] - factor * pivots[i]
    return work


def modes_kernel(count, mine_ref, other_ref, edge_h_ref, edge_l_ref, *refs):
    parts, (out_ref, factor_ref, h_ref, l_ref, wide_ref, corner_ref, buffer, sems, in_sems) = refs[:4], refs[4:]
    loads, start = [], 0
    for k in range(2):
        width = parts[2 * k].shape[0]
        loads.append(
            [
                pltpu.make_async_copy(parts[2 * k + j], ref.at[pl.ds(start, width)], in_sems.at[2 * k + j])
                for j, ref in enumerate((h_ref, l_ref))
            ]
        )
        for load in loads[-1]:
            load.start()
        start += width
    cut = 2 * NX

    @pl.when(lax.axis_index("stream") >= 0)
    def _():
        first = lax.axis_index("span") == 0
        top = jnp.where(first, mine_ref[...], other_ref[...])
        bottom = jnp.where(first, other_ref[...], mine_ref[...])
        groups = [top, pltpu.roll(top, NX - 16, axis=1), pltpu.roll(top, NX - 32, axis=1)]
        groups += [pltpu.roll(top, NX - 64, axis=1), bottom, pltpu.roll(bottom, NX - 48, axis=1)]
        shape = (S, NX)
        row = lax.broadcasted_iota(jnp.int32, shape, 0)
        lane = lax.broadcasted_iota(jnp.int32, shape, 1)
        raw = jnp.concatenate(groups, axis=0) / count
        below = jnp.where(lane < row, raw, 0.0)
        square = jnp.concatenate([below, jnp.zeros((NX - S, NX), F32)], axis=0)
        work = jnp.where(lane <= row, raw, 0.0) + square.T[:S] + jnp.where(lane == row + NX // 2, 1.0, 0.0)
        work = jnp.concatenate(eliminate([work[g * SUB : (g + 1) * SUB] for g in range(S // SUB)]), axis=0)
        diagonal = jnp.sum(jnp.where(lane == row, work, 0.0), axis=1, keepdims=True)
        work = work * lax.rsqrt(diagonal)
        factor_ref[...] = jnp.where(lane >= row, work, 0.0)[:, :S]
        inverse = jnp.where(lane <= row, pltpu.roll(work, NX // 2, axis=1), 0.0)
        high = inverse.astype(BF16).astype(F32)
        both = jnp.concatenate([high, inverse - high], axis=0).astype(BF16)
        wide = lax.dot_general(both, lane_fold().astype(BF16), NT, preferred_element_type=F32)
        same = same_cell()
        tall_high, tall_low = (
            jnp.where(same, jnp.broadcast_to(part[:, None, :], (S, SUB, R)).reshape(R, R), 0.0)
            for part in (wide[:S], wide[S:])
        )
        half = 0.5 * tall_high
        wide_ref[...] = jnp.concatenate([m[:, :cut] for m in (tall_high, tall_low, half)], axis=1).astype(BF16)
        corner = jnp.concatenate(
            [
                jnp.concatenate([tall_high[cut:, cut:], half[cut:, cut:]], axis=1),
                jnp.concatenate([tall_low[cut:, cut:], jnp.zeros((R - cut, R - cut), F32)], axis=1),
            ],
            axis=0,
        )
        corner_ref[...] = corner.astype(BF16)

    slots = buffer.shape[0]

    group = 4

    def copy_out(place):
        q = place - group
        c = jnp.where(q < 0, place // 2, jnp.where(q < 6, 0, jnp.where(q < 12, 1, 2)))
        z = jnp.where(q < 0, place % 2 * (NZ - 1), jnp.where(q < 12, q % 6 + 1, q - 12))
        slot = place % slots
        return pltpu.make_async_copy(buffer.at[slot], out_ref.at[c, :, z], sems.at[slot])

    def apply(step, carry, source=None):
        first = step * group
        if source is None:
            source = (h_ref, l_ref)
            start = first - group

            @pl.when(step >= slots // group)
            def _():
                for k in range(group):
                    copy_out(first + k - slots).wait()
        else:
            start = 0

        for k in range(group):
            h, l = (ref[start + k] for ref in source)
            part = jnp.dot(
                wide_ref[...], jnp.concatenate([h[:cut], h[:cut], l[:cut]], axis=0), preferred_element_type=F32
            )
            last = jnp.dot(
                corner_ref[...], jnp.concatenate([h[cut:], l[cut:]], axis=0), preferred_element_type=F32
            )
            last = part[cut:] + last[: R - cut] + last[R - cut :]
            for value, low in ((part[:cut], 0), (last, cut // SUB)):
                rows = value.shape[0] // SUB
                for half in range(2):
                    tile = value[:, half * NX : (half + 1) * NX].reshape(rows, SUB, NX)
                    buffer[(first + k) % slots, low : low + rows, half * SUB : (half + 1) * SUB, :] = tile
        for k in range(group):
            copy_out(first + k).start()
        return carry

    lax.fori_loop(0, 1, lambda step, carry: apply(0, carry, (edge_h_ref, edge_l_ref)), 0)
    for pair, low, high in zip(loads, (1, 2), (2, 6)):
        for load in pair:
            load.wait()
        lax.fori_loop(low, high, apply, 0)
    for place in range(24 - slots, 24):
        copy_out(place).wait()


def modes_and_factor(mine, other, edge_halves, halves, count):
    return pl.pallas_call(
        functools.partial(modes_kernel, count),
        name="modes",
        out_shape=(
            pltpu.HBM((3, S, NZ, NY, NX), F32),
            jax.ShapeDtypeStruct((S, S), F32),
        ),
        in_specs=[vmem_spec()] * 4 + [any_spec()] * 4,
        out_specs=(any_spec(), vmem_spec()),
        scratch_shapes=[pltpu.VMEM((20, R, PAIR), BF16)] * 2
        + [pltpu.VMEM((R, 6 * NX), BF16), pltpu.VMEM((2 * NX, 2 * NX), BF16)]
        + [pltpu.VMEM((12, S, NY, NX), F32), pltpu.SemaphoreType.DMA((12,)), pltpu.SemaphoreType.DMA((4,))],
        compiler_params=params(24),
    )(*in_vmem(mine, other, *edge_halves), *(in_hbm(h) for h in halves))


def ring(axis, shift):
    count = lax.axis_size(axis)
    return [(i, (i + shift) % count) for i in range(count)]


def total_over_devices(mine, other):
    swap = ring("span", 1)
    mine = mine + lax.ppermute(other, "span", swap)
    axes = ("stream", "vert")
    peers = lax.axis_size(axes)
    mine = lax.all_to_all(jnp.broadcast_to(mine, (peers,) + mine.shape), axes, 0, 0).sum(0)
    return mine, lax.ppermute(mine, "span", swap)


def per_device(velocity):
    v = velocity.reshape(3, S, ROWS, NX)
    head, tail = vertical_faces(v)
    below = lax.ppermute(tail, "vert", ring("vert", 1))
    above = lax.ppermute(head, "vert", ring("vert", -1))
    xs, ys = side_faces(v)
    hy = lax.ppermute(ys, "span", ring("span", 1))
    left = lax.ppermute(xs, "stream", ring("stream", 1))
    right = lax.ppermute(xs, "stream", ring("stream", -1))
    *head_halves, wy, acc = first_component(v, hy)
    *rest_halves, wx, acc = other_components(v, hy, left, right, acc)
    *edge_halves, mine, other = boundary(v, wy, wx, below, above, acc)
    mine, other = total_over_devices(mine, other)
    devices = lax.axis_size("stream") * lax.axis_size("span") * lax.axis_size("vert")
    count = float(3 * NZ * NY * NX * devices)
    return modes_and_factor(mine, other, edge_halves, head_halves + rest_halves, count)


def solution(mesh):
    spec = P(None, None, "vert", "span", "stream")
    return jax.shard_map(per_device, mesh=mesh, in_specs=(spec,), out_specs=(spec, P()), check_vma=False)
```

```python
import functools

import jax
import jax.numpy as jnp
from jax import lax
from jax.experimental import pallas as pl
from jax.experimental.pallas import tpu as pltpu
from jax.sharding import PartitionSpec as P

F32, BF16 = jnp.float32, jnp.bfloat16
HIGH = lax.Precision.HIGHEST
S, NZ, NY, NX = 48, 8, 16, 128
ROWS = NZ * NY
SUB = 8
R = S * SUB
PAIR = 2 * NX
MIB = 1 << 20
NT = (((1,), (1,)), ((), ()))


def any_spec():
    return pl.BlockSpec(memory_space=pl.ANY)


def vmem_spec():
    return pl.BlockSpec(memory_space=pltpu.VMEM)


def params(limit):
    return pltpu.CompilerParams(vmem_limit_bytes=limit * MIB)


def in_vmem(*arrays):
    return [pltpu.with_memory_space_constraint(a, pltpu.VMEM) for a in arrays]


def in_hbm(array):
    return pltpu.with_memory_space_constraint(array, pltpu.HBM)


def vertical_faces_kernel(v_ref, one_ref, two_ref, sems):
    odd = lax.axis_index("vert") % 2
    high = ROWS - NY
    part = S // 2
    copies = []
    for row, ref in (((1 - odd) * high, one_ref), (odd * high, two_ref)):
        rows = pl.ds(pl.multiple_of(row, NY), NY)
        for c in range(2):
            for start in range(0, S, part):
                snaps = pl.ds(start, part)
                copies.append(
                    pltpu.make_async_copy(v_ref.at[c, snaps, rows], ref.at[c, snaps], sems.at[len(copies)])
                )
    for copy in copies:
        copy.start()
    for copy in copies:
        copy.wait()


def vertical_faces(v):
    face = pltpu.VMEM((2, S, NY, NX), F32)
    return pl.pallas_call(
        vertical_faces_kernel,
        name="vertical_faces",
        out_shape=(face, face),
        in_specs=[any_spec()],
        out_specs=(vmem_spec(), vmem_spec()),
        scratch_shapes=[pltpu.SemaphoreType.DMA((8,))],
        compiler_params=params(8),
    )(in_hbm(v))


def side_faces_kernel(block_ref, x_ref, y_ref):
    lane = lax.broadcasted_iota(jnp.int32, (NY, NX), 1) // 2
    for c in (1, 2):

        def pack(z, carry, c=c):
            rows = pl.ds(pl.multiple_of(z * NY, NY), NY)
            packed = jnp.zeros((NY, NX), F32)
            for s in range(S):
                turned = pltpu.roll(block_ref[c, s, rows, :], 2 * s + 1, axis=1)
                packed = jnp.where(lane == s, turned, packed)
            x_ref[c - 1, rows, :] = packed
            return carry

        lax.fori_loop(0, NZ, pack, 0)
    first = lax.axis_index("span") == 0
    for k, c in enumerate((0, 2)):
        for s in range(S):
            high = block_ref[c, s, pl.ds(NY - 1, NZ, stride=NY), :]
            low = block_ref[c, s, pl.ds(0, NZ, stride=NY), :]
            y_ref[k, s] = jnp.where(first, high, low)


def side_faces(block):
    return pl.pallas_call(
        side_faces_kernel,
        name="side_faces",
        out_shape=(
            pltpu.VMEM((2, ROWS, NX), F32),
            pltpu.VMEM((2, S, NZ, NX), F32),
        ),
        in_specs=[vmem_spec()],
        out_specs=(vmem_spec(), vmem_spec()),
        compiler_params=params(8),
    )(*in_vmem(block))


def split_store(first, second, pair, place, h_ref, l_ref):
    for half in range(2):
        rows = slice(half * SUB, (half + 1) * SUB)
        value = jnp.concatenate([first[rows], second[rows]], axis=0)
        high = value.astype(BF16)
        low = ((value - high.astype(F32)) * 2.0).astype(BF16)
        where = (place, pl.ds(pair * 2 * SUB, 2 * SUB), pl.ds(half * NX, NX))
        h_ref[where] = high
        l_ref[where] = low


def products(h_ref, l_ref, places):
    highs, lows = [h_ref[p] for p in places], [l_ref[p] for p in places]
    left, right = jnp.concatenate(highs + highs, axis=1), jnp.concatenate(highs + lows, axis=1)
    return lax.dot_general(left, right, NT, preferred_element_type=F32)


def level(s, z):
    return slice(s * ROWS + z * NY, s * ROWS + (z + 1) * NY)


def slope_z(v_ref, c, s, z):
    return v_ref[c, level(s, z + 1), :] - v_ref[c, level(s, z - 1), :]


def slope_y(v_ref, hy_ref, c, s, z):
    row = lax.broadcasted_iota(jnp.int32, (NY, NX), 0)
    first = lax.axis_index("span") == 0
    base = s * ROWS + z * NY

    def rows(start):
        inside = min(max(start, 0), S * ROWS - SUB)
        part = v_ref[c, inside : inside + SUB, :]
        return part if inside == start else pltpu.roll(part, (inside - start) % SUB, axis=0)

    def shifted(by):
        return jnp.concatenate([rows(base + by), rows(base + SUB + by)], axis=0)

    face = hy_ref[c // 2, s, z : z + 1, :]
    up = jnp.where(row == NY - 1, jnp.where(first, face, 0.0), shifted(1))
    down = jnp.where(row == 0, jnp.where(first, 0.0, face), shifted(-1))
    return up - down


def lanes():
    return lax.broadcasted_iota(jnp.int32, (NY, NX), 1)


def inner_slope_x(v_ref, c, s, z):
    cells = v_ref[c, level(s, z), :]
    up = jnp.where(lanes() == NX - 1, 0.0, pltpu.roll(cells, NX - 1, axis=1))
    down = jnp.where(lanes() == 0, 0.0, pltpu.roll(cells, 1, axis=1))
    return up - down


def edge_slope_x(edge_ref, k, s, z):
    edge = edge_ref[k, level(0, z), :]
    if s:
        edge = pltpu.roll(edge, NX - 2 * s, axis=1)
    return jnp.where((lanes() == 0) | (lanes() == NX - 1), edge, 0.0)


def send_out(places, scratch, refs, sems):
    for i, (a, b) in enumerate(zip(scratch, refs)):
        for p in places:
            pltpu.make_async_copy(a.at[p], b.at[p], sems.at[i]).start()


def wait_out(scratch, refs, sems):
    for i, (a, b) in enumerate(zip(scratch, refs)):
        pltpu.make_async_copy(a, b, sems.at[i]).wait()


def first_kernel(v_ref, hy_ref, h_out, l_out, part_ref, wx_ref, acc_ref, h_ref, l_ref, sems):
    def vorticity(z):
        for s in range(0, S, 2):
            pair = (0.5 * (slope_y(v_ref, hy_ref, 2, t, z) - slope_z(v_ref, 1, t, z)) for t in (s, s + 1))
            split_store(*pair, s // 2, z - 1, h_ref, l_ref)
        send_out([z - 1], (h_ref, l_ref), (h_out, l_out), sems)

    def slopes(z):
        for s in range(S):
            wx_ref[level(s, z), :] = inner_slope_x(v_ref, 2, s, z)

    vorticity(1)
    slopes(0)
    slopes(1)
    vorticity(2)
    slopes(2)
    acc_ref[...] = products(h_ref, l_ref, [0])
    for z in range(3, NZ - 1):
        vorticity(z)
        slopes(z)
        acc_ref[...] += products(h_ref, l_ref, [z - 2])
    for k in range(2):
        for s in range(S):
            part_ref[k, s] = slope_y(v_ref, hy_ref, 2, s, k * (NZ - 1))
    slopes(NZ - 1)
    acc_ref[...] += products(h_ref, l_ref, [NZ - 3])

    @pl.when(lax.axis_index("span") >= 0)
    def _():
        wait_out((h_ref, l_ref), (h_out, l_out), sems)

def first_component(block, hy):
    block = block.reshape(3, S * ROWS, NX)
    half = pltpu.HBM((6, R, PAIR), BF16)
    return pl.pallas_call(
        first_kernel,
        name="first_component",
        out_shape=(
            half,
            half,
            pltpu.VMEM((2, S, NY, NX), F32),
            pltpu.VMEM((S * ROWS, NX), F32),
            pltpu.VMEM((R, R), F32),
        ),
        in_specs=[vmem_spec()] * 2,
        out_specs=(any_spec(), any_spec(), vmem_spec(), vmem_spec(), vmem_spec()),
        scratch_shapes=[pltpu.VMEM((6, R, PAIR), BF16)] * 2 + [pltpu.SemaphoreType.DMA((2,))],
        compiler_params=params(8),
        cost_estimate=pl.CostEstimate(flops=4 * R * R * 6 * PAIR, bytes_accessed=6 * MIB, transcendentals=0),
    )(*in_vmem(block, hy))


def rest_kernel(
    v_ref, hy_ref, even_ref, odd_ref, wx_ref, old_ref, h_out, l_out, part_ref, acc_ref, h_last, l_last,
    edge_ref, h_ref, l_ref, sems
):
    lane = lanes()
    stream = lax.axis_index("stream")
    even = stream % 2 == 0
    for c in range(2):
        for z in range(NZ):
            rows = pl.ds(z * NY, NY)
            one, two = even_ref[c, rows, :], odd_ref[c, rows, :]
            left, right = jnp.where(even, two, one), jnp.where(even, one, two)
            before = jnp.where(stream > 0, left, 0.0)
            behind = jnp.where(stream < lax.axis_size("stream") - 1, right, 0.0)
            edge_ref[c, rows, :] = jnp.where(lane % 2 == 0, -before, pltpu.roll(behind, NX - 2, axis=1))

    def slope_wx(s, z):
        return wx_ref[level(s, z), :] + edge_slope_x(edge_ref, 1, s, z)

    def second(z):
        for s in range(0, S, 2):
            pair = (0.5 * (slope_z(v_ref, 0, t, z) - slope_wx(t, z)) for t in (s, s + 1))
            split_store(*pair, s // 2, z - 1, h_ref, l_ref)
        send_out([z - 1], (h_ref, l_ref), (h_out, l_out), sems)

    def third(z):
        for s in range(0, S, 2):
            pair = (
                0.5
                * (inner_slope_x(v_ref, 1, t, z) + edge_slope_x(edge_ref, 0, t, z) - slope_y(v_ref, hy_ref, 0, t, z))
                for t in (s, s + 1)
            )
            if z < NZ - 2:
                split_store(*pair, s // 2, z + 6, h_ref, l_ref)
            else:
                split_store(*pair, s // 2, z - NZ + 2, h_last, l_last)
        if z < NZ - 2:
            send_out([z + 6], (h_ref, l_ref), (h_out, l_out), sems)

    third(0)
    second(1)
    third(1)
    acc_ref[...] = old_ref[...] + products(h_ref, l_ref, [6])
    for z in range(2, NZ - 1):
        second(z)
        third(z)
        acc_ref[...] += products(h_ref, l_ref, [z - 2, z + 5])
    third(NZ - 1)
    acc_ref[...] += products(h_ref, l_ref, [NZ - 3])
    for k in range(2):
        for s in range(S):
            part_ref[k, s] = slope_wx(s, k * (NZ - 1))
    acc_ref[...] += products(h_last, l_last, range(2))

    @pl.when(stream >= 0)
    def _():
        wait_out((h_ref, l_ref), (h_out, l_out), sems)


def other_components(block, hy, even, odd, wx, acc):
    block = block.reshape(3, S * ROWS, NX)
    half, last = pltpu.HBM((12, R, PAIR), BF16), pltpu.VMEM((2, R, PAIR), BF16)
    return pl.pallas_call(
        rest_kernel,
        name="other_components",
        out_shape=(half, half, pltpu.VMEM((2, S, NY, NX), F32), pltpu.VMEM((R, R), F32), last, last),
        in_specs=[vmem_spec()] * 6,
        out_specs=(any_spec(), any_spec()) + (vmem_spec(),) * 4,
        scratch_shapes=[pltpu.VMEM((2, ROWS, NX), F32)]
        + [pltpu.VMEM((12, R, PAIR), BF16)] * 2
        + [pltpu.SemaphoreType.DMA((2,))],
        compiler_params=params(12),
        cost_estimate=pl.CostEstimate(flops=4 * R * R * 14 * PAIR, bytes_accessed=12 * MIB, transcendentals=0),
    )(*in_vmem(block, hy, even, odd, wx, acc))


def lane_fold():
    shape = (R, NX)
    same = lax.broadcasted_iota(jnp.int32, shape, 0) // SUB == lax.broadcasted_iota(jnp.int32, shape, 1)
    return jnp.where(same, 1.0, 0.0)


def same_cell():
    return lax.broadcasted_iota(jnp.int32, (R, R), 0) % SUB == lax.broadcasted_iota(jnp.int32, (R, R), 1) % SUB


def boundary_kernel(
    v_ref, wy_ref, wx_ref, one_ref, two_ref, acc_ref, h_ref, l_ref, mine_ref, other_ref, sum_ref
):
    vert = lax.axis_index("vert")
    has_below, has_above = vert > 0, vert < lax.axis_size("vert") - 1

    def vorticity(below_ref, above_ref):
        def dz(c, s, k):
            if k:
                return jnp.where(has_above, above_ref[c, s], 0.0) - v_ref[c, s, pl.ds((NZ - 2) * NY, NY), :]
            return v_ref[c, s, pl.ds(NY, NY), :] - jnp.where(has_below, below_ref[c, s], 0.0)

        for k in range(2):
            for s in range(0, S, 2):
                first = (0.5 * (wy_ref[k, t] - dz(1, t, k)) for t in (s, s + 1))
                split_store(*first, s // 2, k, h_ref, l_ref)
        for k in range(2):
            for s in range(0, S, 2):
                second = (0.5 * (dz(0, t, k) - wx_ref[k, t]) for t in (s, s + 1))
                split_store(*second, s // 2, 2 + k, h_ref, l_ref)
            if not k:
                sum_ref[...] = acc_ref[...] + products(h_ref, l_ref, range(2))
        sum_ref[...] += products(h_ref, l_ref, range(2, 4))

    @pl.when(vert % 2 == 0)
    def _():
        vorticity(two_ref, one_ref)

    @pl.when(vert % 2 == 1)
    def _():
        vorticity(one_ref, two_ref)

    total = sum_ref[...]
    total = jnp.where(same_cell(), total, 0.0).reshape(S, SUB, R).sum(1)
    total = lax.dot_general(
        total, lane_fold(), (((1,), (0,)), ((), ())), precision=HIGH, preferred_element_type=F32
    )
    square = jnp.concatenate([total, jnp.zeros((NX - S, NX), F32)], axis=0)
    total = 0.5 * (total + square.T[:S])
    lane = lax.broadcasted_iota(jnp.int32, (SUB, NX), 1)
    groups = [total[g * SUB : (g + 1) * SUB] for g in range(S // SUB)]
    bottom = jnp.where(lane < 48, groups[4], pltpu.roll(groups[5], 48, axis=1))
    top = jnp.where(lane < 64, pltpu.roll(groups[2], 32, axis=1), pltpu.roll(groups[3], 64, axis=1))
    top = jnp.where(lane < 16, groups[0], jnp.where(lane < 32, pltpu.roll(groups[1], 16, axis=1), top))
    first = lax.axis_index("span") == 0
    mine_ref[...] = jnp.where(first, top, bottom)
    other_ref[...] = jnp.where(first, bottom, top)


def boundary(block, wy, wx, one, two, acc):
    half = pltpu.VMEM((4, R, PAIR), BF16)
    sums = pltpu.VMEM((SUB, NX), F32)
    return pl.pallas_call(
        boundary_kernel,
        name="boundary",
        out_shape=(half, half, sums, sums),
        in_specs=[vmem_spec()] * 6,
        out_specs=(vmem_spec(),) * 4,
        scratch_shapes=[pltpu.VMEM((R, R), F32)],
        compiler_params=params(8),
    )(*in_vmem(block, wy, wx, one, two, acc))


def eliminate(work):
    row = lax.broadcasted_iota(jnp.int32, (SUB, NX), 0)

    def spread(part):
        return jnp.broadcast_to(part, (SUB, NX))

    width = SUB
    for start in range(0, S, width):
        home, base = start // SUB, start % SUB
        live = range(home, S // SUB)
        pivots = [spread(work[home][base + j : base + j + 1, :]) for j in range(width)]
        cols = [{g: spread(work[g][:, start + j : start + j + 1]) for g in live} for j in range(width)]
        heads = [[spread(cols[j][home][base + i : base + i + 1, :]) for j in range(width)] for i in range(width)]
        for i in range(width):
            scale = 1.0 / heads[i][i]
            for j in range(i + 1, width):
                ratio = heads[i][j] * scale
                pivots[j] = pivots[j] - ratio * pivots[i]
                for g in live:
                    cols[j][g] = cols[j][g] - ratio * cols[i][g]
                for k in range(j, width):
                    heads[j][k] = heads[j][k] - ratio * heads[i][k]
            for g in live:
                factor = cols[i][g] * scale
                if g == home:
                    factor = jnp.where(row > base + i, factor, 0.0)
                work[g] = work[g] - factor * pivots[i]
    return work


def modes_kernel(count, mine_ref, other_ref, edge_h_ref, edge_l_ref, last_h_ref, last_l_ref, *refs):
    parts, (out_ref, factor_ref, h_ref, l_ref, wide_ref, corner_ref, buffer, sems, in_sems) = refs[:4], refs[4:]
    loads, start = [], 0
    for k in range(2):
        width = parts[2 * k].shape[0]
        loads.append(
            [
                pltpu.make_async_copy(parts[2 * k + j], ref.at[pl.ds(start, width)], in_sems.at[2 * k + j])
                for j, ref in enumerate((h_ref, l_ref))
            ]
        )
        for load in loads[-1]:
            load.start()
        start += width
    cut = 2 * NX

    @pl.when(lax.axis_index("stream") >= 0)
    def _():
        first = lax.axis_index("span") == 0
        top = jnp.where(first, mine_ref[...], other_ref[...])
        bottom = jnp.where(first, other_ref[...], mine_ref[...])
        groups = [top, pltpu.roll(top, NX - 16, axis=1), pltpu.roll(top, NX - 32, axis=1)]
        groups += [pltpu.roll(top, NX - 64, axis=1), bottom, pltpu.roll(bottom, NX - 48, axis=1)]
        shape = (S, NX)
        row = lax.broadcasted_iota(jnp.int32, shape, 0)
        lane = lax.broadcasted_iota(jnp.int32, shape, 1)
        raw = jnp.concatenate(groups, axis=0) / count
        below = jnp.where(lane < row, raw, 0.0)
        square = jnp.concatenate([below, jnp.zeros((NX - S, NX), F32)], axis=0)
        work = jnp.where(lane <= row, raw, 0.0) + square.T[:S] + jnp.where(lane == row + NX // 2, 1.0, 0.0)
        work = jnp.concatenate(eliminate([work[g * SUB : (g + 1) * SUB] for g in range(S // SUB)]), axis=0)
        diagonal = jnp.sum(jnp.where(lane == row, work, 0.0), axis=1, keepdims=True)
        work = work * lax.rsqrt(diagonal)
        factor_ref[...] = jnp.where(lane >= row, work, 0.0)[:, :S]
        inverse = jnp.where(lane <= row, pltpu.roll(work, NX // 2, axis=1), 0.0)
        high = inverse.astype(BF16).astype(F32)
        both = jnp.concatenate([high, inverse - high], axis=0).astype(BF16)
        wide = lax.dot_general(both, lane_fold().astype(BF16), NT, preferred_element_type=F32)
        same = same_cell()
        tall_high, tall_low = (
            jnp.where(same, jnp.broadcast_to(part[:, None, :], (S, SUB, R)).reshape(R, R), 0.0)
            for part in (wide[:S], wide[S:])
        )
        half = 0.5 * tall_high
        wide_ref[...] = jnp.concatenate([m[:, :cut] for m in (tall_high, tall_low, half)], axis=1).astype(BF16)
        corner = jnp.concatenate(
            [
                jnp.concatenate([tall_high[cut:, cut:], half[cut:, cut:]], axis=1),
                jnp.concatenate([tall_low[cut:, cut:], jnp.zeros((R - cut, R - cut), F32)], axis=1),
            ],
            axis=0,
        )
        corner_ref[...] = corner.astype(BF16)

    slots = buffer.shape[0]

    group = 6

    def copy_out(place):
        q = place - group
        c = jnp.where(q < 0, place // 2, jnp.where(q < 6, 0, jnp.where(q < 12, 1, 2)))
        z = jnp.where(place < 4, place % 2 * (NZ - 1), jnp.where(q < 0, place + 2, jnp.where(q < 12, q % 6 + 1, q - 12)))
        slot = place % slots
        return pltpu.make_async_copy(buffer.at[slot], out_ref.at[c, :, z], sems.at[slot])

    def held(k):
        if k < 4:
            return edge_h_ref[k], edge_l_ref[k]
        return last_h_ref[k - 4], last_l_ref[k - 4]

    def apply(step, carry, source=None):
        first = step * group
        if source is None:

            @pl.when(step >= slots // group)
            def _():
                for k in range(group):
                    copy_out(first + k - slots).wait()

            def source(k):
                return h_ref[first - group + k], l_ref[first - group + k]

        for k in range(group):
            h, l = source(k)
            part = jnp.dot(
                wide_ref[...], jnp.concatenate([h[:cut], h[:cut], l[:cut]], axis=0), preferred_element_type=F32
            )
            last = jnp.dot(
                corner_ref[...], jnp.concatenate([h[cut:], l[cut:]], axis=0), preferred_element_type=F32
            )
            last = part[cut:] + last[: R - cut] + last[R - cut :]
            for value, low in ((part[:cut], 0), (last, cut // SUB)):
                rows = value.shape[0] // SUB
                for half in range(2):
                    tile = value[:, half * NX : (half + 1) * NX].reshape(rows, SUB, NX)
                    buffer[(first + k) % slots, low : low + rows, half * SUB : (half + 1) * SUB, :] = tile
            copy_out(first + k).start()
        return carry

    lax.fori_loop(0, 1, lambda step, carry: apply(0, carry, held), 0)
    for pair, low, high in zip(loads, (1, 2), (2, 4)):
        for load in pair:
            load.wait()
        lax.fori_loop(low, high, apply, 0)
    for place in range(24 - slots, 24):
        copy_out(place).wait()


def modes_and_factor(mine, other, held, halves, count):
    return pl.pallas_call(
        functools.partial(modes_kernel, count),
        name="modes",
        out_shape=(
            pltpu.HBM((3, S, NZ, NY, NX), F32),
            jax.ShapeDtypeStruct((S, S), F32),
        ),
        in_specs=[vmem_spec()] * 6 + [any_spec()] * 4,
        out_specs=(any_spec(), vmem_spec()),
        scratch_shapes=[pltpu.VMEM((18, R, PAIR), BF16)] * 2
        + [pltpu.VMEM((R, 6 * NX), BF16), pltpu.VMEM((2 * NX, 2 * NX), BF16)]
        + [pltpu.VMEM((12, S, NY, NX), F32), pltpu.SemaphoreType.DMA((12,)), pltpu.SemaphoreType.DMA((4,))],
        compiler_params=params(24),
    )(*in_vmem(mine, other, *held), *(in_hbm(h) for h in halves))


def ring(axis, shift):
    count = lax.axis_size(axis)
    return [(i, (i + shift) % count) for i in range(count)]


def neighbours(axis, first):
    count = lax.axis_size(axis)
    pairs = [(i, (i + 1) % count) for i in range(first, count, 2)]
    return pairs + [(b, a) for a, b in pairs]


def total_over_devices(mine, other):
    swap = ring("span", 1)
    mine = mine + lax.ppermute(other, "span", swap)
    axes = ("stream", "vert")
    peers = lax.axis_size(axes)
    mine = lax.all_to_all(jnp.broadcast_to(mine, (peers,) + mine.shape), axes, 0, 0).sum(0)
    return mine, lax.ppermute(mine, "span", swap)


def per_device(velocity):
    v = velocity.reshape(3, S, ROWS, NX)
    one, two = vertical_faces(v)
    one = lax.ppermute(one, "vert", neighbours("vert", 0))
    two = lax.ppermute(two, "vert", neighbours("vert", 1))
    xs, ys = side_faces(v)
    hy = lax.ppermute(ys, "span", ring("span", 1))
    even = lax.ppermute(xs, "stream", neighbours("stream", 0))
    odd = lax.ppermute(xs, "stream", neighbours("stream", 1))
    *head_halves, wy, wx, acc = first_component(v, hy)
    *rest_halves, wx, acc, last_high, last_low = other_components(v, hy, even, odd, wx, acc)
    *edge_halves, mine, other = boundary(v, wy, wx, one, two, acc)
    mine, other = total_over_devices(mine, other)
    devices = lax.axis_size("stream") * lax.axis_size("span") * lax.axis_size("vert")
    count = float(3 * NZ * NY * NX * devices)
    return modes_and_factor(
        mine, other, edge_halves + [last_high, last_low], head_halves + rest_halves, count
    )


def solution(mesh):
    spec = P(None, None, "vert", "span", "stream")
    return jax.shard_map(per_device, mesh=mesh, in_specs=(spec,), out_specs=(spec, P()), check_vma=False)
```

```python
import functools

import jax
import jax.numpy as jnp
from jax import lax
from jax.experimental import pallas as pl
from jax.experimental.pallas import tpu as pltpu
from jax.sharding import PartitionSpec as P

F32, BF16 = jnp.float32, jnp.bfloat16
HIGH = lax.Precision.HIGHEST
S, NZ, NY, NX = 48, 8, 16, 128
ROWS = NZ * NY
SUB = 8
R = S * SUB
PAIR = 2 * NX
MIB = 1 << 20
NT = (((1,), (1,)), ((), ()))


def any_spec():
    return pl.BlockSpec(memory_space=pl.ANY)


def vmem_spec():
    return pl.BlockSpec(memory_space=pltpu.VMEM)


def params(limit):
    return pltpu.CompilerParams(vmem_limit_bytes=limit * MIB)


def in_vmem(*arrays):
    return [pltpu.with_memory_space_constraint(a, pltpu.VMEM) for a in arrays]


def in_hbm(array):
    return pltpu.with_memory_space_constraint(array, pltpu.HBM)


def vertical_faces_kernel(v_ref, one_ref, two_ref, sems):
    odd = lax.axis_index("vert") % 2
    high = ROWS - NY
    part = S // 2
    copies = []
    for row, ref in (((1 - odd) * high, one_ref), (odd * high, two_ref)):
        rows = pl.ds(pl.multiple_of(row, NY), NY)
        for c in range(2):
            for start in range(0, S, part):
                snaps = pl.ds(start, part)
                copies.append(
                    pltpu.make_async_copy(v_ref.at[c, snaps, rows], ref.at[c, snaps], sems.at[len(copies)])
                )
    for copy in copies:
        copy.start()
    for copy in copies:
        copy.wait()


def vertical_faces(v):
    face = pltpu.VMEM((2, S, NY, NX), F32)
    return pl.pallas_call(
        vertical_faces_kernel,
        name="vertical_faces",
        out_shape=(face, face),
        in_specs=[any_spec()],
        out_specs=(vmem_spec(), vmem_spec()),
        scratch_shapes=[pltpu.SemaphoreType.DMA((8,))],
        compiler_params=params(8),
    )(in_hbm(v))


def side_faces_kernel(block_ref, x_ref, y_ref):
    lane = lax.broadcasted_iota(jnp.int32, (NY, NX), 1) // 2
    for c in (1, 2):

        def pack(z, carry, c=c):
            rows = pl.ds(pl.multiple_of(z * NY, NY), NY)
            packed = jnp.zeros((NY, NX), F32)
            for s in range(S):
                turned = pltpu.roll(block_ref[c, s, rows, :], 2 * s + 1, axis=1)
                packed = jnp.where(lane == s, turned, packed)
            x_ref[c - 1, rows, :] = packed
            return carry

        lax.fori_loop(0, NZ, pack, 0)
    first = lax.axis_index("span") == 0
    for k, c in enumerate((0, 2)):
        for s in range(S):
            high = block_ref[c, s, pl.ds(NY - 1, NZ, stride=NY), :]
            low = block_ref[c, s, pl.ds(0, NZ, stride=NY), :]
            y_ref[k, s] = jnp.where(first, high, low)


def side_faces(block):
    return pl.pallas_call(
        side_faces_kernel,
        name="side_faces",
        out_shape=(
            pltpu.VMEM((2, ROWS, NX), F32),
            pltpu.VMEM((2, S, NZ, NX), F32),
        ),
        in_specs=[vmem_spec()],
        out_specs=(vmem_spec(), vmem_spec()),
        compiler_params=params(8),
    )(*in_vmem(block))


def split_store(first, second, pair, place, h_ref, l_ref):
    for half in range(2):
        rows = slice(half * SUB, (half + 1) * SUB)
        value = jnp.concatenate([first[rows], second[rows]], axis=0)
        high = value.astype(BF16)
        low = ((value - high.astype(F32)) * 2.0).astype(BF16)
        where = (place, pl.ds(pair * 2 * SUB, 2 * SUB), pl.ds(half * NX, NX))
        h_ref[where] = high
        l_ref[where] = low


def products(h_ref, l_ref, places):
    highs, lows = [h_ref[p] for p in places], [l_ref[p] for p in places]
    left, right = jnp.concatenate(highs + highs, axis=1), jnp.concatenate(highs + lows, axis=1)
    return lax.dot_general(left, right, NT, preferred_element_type=F32)


def level(s, z):
    return slice(s * ROWS + z * NY, s * ROWS + (z + 1) * NY)


def slope_z(v_ref, c, s, z):
    return v_ref[c, level(s, z + 1), :] - v_ref[c, level(s, z - 1), :]


def slope_y(v_ref, hy_ref, c, s, z):
    row = lax.broadcasted_iota(jnp.int32, (NY, NX), 0)
    first = lax.axis_index("span") == 0
    base = s * ROWS + z * NY

    def rows(start):
        inside = min(max(start, 0), S * ROWS - SUB)
        part = v_ref[c, inside : inside + SUB, :]
        return part if inside == start else pltpu.roll(part, (inside - start) % SUB, axis=0)

    def shifted(by):
        return jnp.concatenate([rows(base + by), rows(base + SUB + by)], axis=0)

    face = hy_ref[c // 2, s, z : z + 1, :]
    up = jnp.where(row == NY - 1, jnp.where(first, face, 0.0), shifted(1))
    down = jnp.where(row == 0, jnp.where(first, 0.0, face), shifted(-1))
    return up - down


def lanes():
    return lax.broadcasted_iota(jnp.int32, (NY, NX), 1)


def inner_slope_x(v_ref, c, s, z):
    cells = v_ref[c, level(s, z), :]
    up = jnp.where(lanes() == NX - 1, 0.0, pltpu.roll(cells, NX - 1, axis=1))
    down = jnp.where(lanes() == 0, 0.0, pltpu.roll(cells, 1, axis=1))
    return up - down


def edge_slope_x(edge_ref, k, s, z):
    edge = edge_ref[k, level(0, z), :]
    if s:
        edge = pltpu.roll(edge, NX - 2 * s, axis=1)
    return jnp.where((lanes() == 0) | (lanes() == NX - 1), edge, 0.0)


def send_out(places, scratch, refs, sems):
    for i, (a, b) in enumerate(zip(scratch, refs)):
        for p in places:
            pltpu.make_async_copy(a.at[p], b.at[p], sems.at[i]).start()


def wait_out(scratch, refs, sems):
    for i, (a, b) in enumerate(zip(scratch, refs)):
        pltpu.make_async_copy(a, b, sems.at[i]).wait()


def first_kernel(v_ref, hy_ref, h_out, l_out, part_ref, wx_ref, acc_ref, h_ref, l_ref, sems):
    def vorticity(z):
        for s in range(0, S, 2):
            pair = (0.5 * (slope_y(v_ref, hy_ref, 2, t, z) - slope_z(v_ref, 1, t, z)) for t in (s, s + 1))
            split_store(*pair, s // 2, z - 1, h_ref, l_ref)
        send_out([z - 1], (h_ref, l_ref), (h_out, l_out), sems)

    def slopes(z):
        for s in range(S):
            wx_ref[level(s, z), :] = inner_slope_x(v_ref, 2, s, z)

    vorticity(1)
    slopes(0)
    slopes(1)
    vorticity(2)
    slopes(2)
    acc_ref[...] = products(h_ref, l_ref, [0])
    for z in range(3, NZ - 1):
        vorticity(z)
        slopes(z)
        acc_ref[...] += products(h_ref, l_ref, [z - 2])
    for k in range(2):
        for s in range(S):
            part_ref[k, s] = slope_y(v_ref, hy_ref, 2, s, k * (NZ - 1))
    slopes(NZ - 1)
    acc_ref[...] += products(h_ref, l_ref, [NZ - 3])

    @pl.when(lax.axis_index("span") >= 0)
    def _():
        wait_out((h_ref, l_ref), (h_out, l_out), sems)

def first_component(block, hy):
    block = block.reshape(3, S * ROWS, NX)
    half = pltpu.HBM((6, R, PAIR), BF16)
    return pl.pallas_call(
        first_kernel,
        name="first_component",
        out_shape=(
            half,
            half,
            pltpu.VMEM((2, S, NY, NX), F32),
            pltpu.VMEM((S * ROWS, NX), F32),
            pltpu.VMEM((R, R), F32),
        ),
        in_specs=[vmem_spec()] * 2,
        out_specs=(any_spec(), any_spec(), vmem_spec(), vmem_spec(), vmem_spec()),
        scratch_shapes=[pltpu.VMEM((6, R, PAIR), BF16)] * 2 + [pltpu.SemaphoreType.DMA((2,))],
        compiler_params=params(8),
        cost_estimate=pl.CostEstimate(flops=4 * R * R * 6 * PAIR, bytes_accessed=6 * MIB, transcendentals=0),
    )(*in_vmem(block, hy))


def rest_kernel(
    v_ref, hy_ref, even_ref, odd_ref, wx_ref, old_ref, h_out, l_out, part_ref, acc_ref, h_last, l_last,
    edge_ref, h_ref, l_ref, sems
):
    lane = lanes()
    stream = lax.axis_index("stream")
    even = stream % 2 == 0
    for c in range(2):
        for z in range(NZ):
            rows = pl.ds(z * NY, NY)
            one, two = even_ref[c, rows, :], odd_ref[c, rows, :]
            left, right = jnp.where(even, two, one), jnp.where(even, one, two)
            before = jnp.where(stream > 0, left, 0.0)
            behind = jnp.where(stream < lax.axis_size("stream") - 1, right, 0.0)
            edge_ref[c, rows, :] = jnp.where(lane % 2 == 0, -before, pltpu.roll(behind, NX - 2, axis=1))

    def slope_wx(s, z):
        return wx_ref[level(s, z), :] + edge_slope_x(edge_ref, 1, s, z)

    def second(z):
        for s in range(0, S, 2):
            pair = (0.5 * (slope_z(v_ref, 0, t, z) - slope_wx(t, z)) for t in (s, s + 1))
            split_store(*pair, s // 2, z - 1, h_ref, l_ref)
        send_out([z - 1], (h_ref, l_ref), (h_out, l_out), sems)

    def third(z):
        for s in range(0, S, 2):
            pair = (
                0.5
                * (inner_slope_x(v_ref, 1, t, z) + edge_slope_x(edge_ref, 0, t, z) - slope_y(v_ref, hy_ref, 0, t, z))
                for t in (s, s + 1)
            )
            if z < NZ - 2:
                split_store(*pair, s // 2, z + 6, h_ref, l_ref)
            else:
                split_store(*pair, s // 2, z - NZ + 2, h_last, l_last)
        if z < NZ - 2:
            send_out([z + 6], (h_ref, l_ref), (h_out, l_out), sems)

    third(0)
    second(1)
    third(1)
    acc_ref[...] = old_ref[...] + products(h_ref, l_ref, [6])
    for z in range(2, NZ - 1):
        second(z)
        third(z)
        acc_ref[...] += products(h_ref, l_ref, [z - 2, z + 5])
    third(NZ - 1)
    acc_ref[...] += products(h_ref, l_ref, [NZ - 3])
    for k in range(2):
        for s in range(S):
            part_ref[k, s] = slope_wx(s, k * (NZ - 1))
    acc_ref[...] += products(h_last, l_last, range(2))

    @pl.when(stream >= 0)
    def _():
        wait_out((h_ref, l_ref), (h_out, l_out), sems)


def other_components(block, hy, even, odd, wx, acc):
    block = block.reshape(3, S * ROWS, NX)
    half, last = pltpu.HBM((12, R, PAIR), BF16), pltpu.VMEM((2, R, PAIR), BF16)
    return pl.pallas_call(
        rest_kernel,
        name="other_components",
        out_shape=(half, half, pltpu.VMEM((2, S, NY, NX), F32), pltpu.VMEM((R, R), F32), last, last),
        in_specs=[vmem_spec()] * 6,
        out_specs=(any_spec(), any_spec()) + (vmem_spec(),) * 4,
        scratch_shapes=[pltpu.VMEM((2, ROWS, NX), F32)]
        + [pltpu.VMEM((12, R, PAIR), BF16)] * 2
        + [pltpu.SemaphoreType.DMA((2,))],
        compiler_params=params(12),
        cost_estimate=pl.CostEstimate(flops=4 * R * R * 14 * PAIR, bytes_accessed=12 * MIB, transcendentals=0),
    )(*in_vmem(block, hy, even, odd, wx, acc))


def lane_fold():
    shape = (R, NX)
    same = lax.broadcasted_iota(jnp.int32, shape, 0) // SUB == lax.broadcasted_iota(jnp.int32, shape, 1)
    return jnp.where(same, 1.0, 0.0)


def same_cell():
    return lax.broadcasted_iota(jnp.int32, (R, R), 0) % SUB == lax.broadcasted_iota(jnp.int32, (R, R), 1) % SUB


def boundary_kernel(
    v_ref, wy_ref, wx_ref, one_ref, two_ref, acc_ref, h_ref, l_ref, mine_ref, other_ref, sum_ref
):
    vert = lax.axis_index("vert")
    has_below, has_above = vert > 0, vert < lax.axis_size("vert") - 1

    def vorticity(below_ref, above_ref):
        def dz(c, s, k):
            if k:
                return jnp.where(has_above, above_ref[c, s], 0.0) - v_ref[c, s, pl.ds((NZ - 2) * NY, NY), :]
            return v_ref[c, s, pl.ds(NY, NY), :] - jnp.where(has_below, below_ref[c, s], 0.0)

        for k in range(2):
            for s in range(0, S, 2):
                first = (0.5 * (wy_ref[k, t] - dz(1, t, k)) for t in (s, s + 1))
                split_store(*first, s // 2, k, h_ref, l_ref)
        for k in range(2):
            for s in range(0, S, 2):
                second = (0.5 * (dz(0, t, k) - wx_ref[k, t]) for t in (s, s + 1))
                split_store(*second, s // 2, 2 + k, h_ref, l_ref)
            if not k:
                sum_ref[...] = acc_ref[...] + products(h_ref, l_ref, range(2))
        sum_ref[...] += products(h_ref, l_ref, range(2, 4))

    @pl.when(vert % 2 == 0)
    def _():
        vorticity(two_ref, one_ref)

    @pl.when(vert % 2 == 1)
    def _():
        vorticity(one_ref, two_ref)

    total = sum_ref[...]
    total = jnp.where(same_cell(), total, 0.0).reshape(S, SUB, R).sum(1)
    total = lax.dot_general(
        total, lane_fold(), (((1,), (0,)), ((), ())), precision=HIGH, preferred_element_type=F32
    )
    square = jnp.concatenate([total, jnp.zeros((NX - S, NX), F32)], axis=0)
    total = 0.5 * (total + square.T[:S])
    lane = lax.broadcasted_iota(jnp.int32, (SUB, NX), 1)
    groups = [total[g * SUB : (g + 1) * SUB] for g in range(S // SUB)]
    bottom = jnp.where(lane < 48, groups[4], pltpu.roll(groups[5], 48, axis=1))
    top = jnp.where(lane < 64, pltpu.roll(groups[2], 32, axis=1), pltpu.roll(groups[3], 64, axis=1))
    top = jnp.where(lane < 16, groups[0], jnp.where(lane < 32, pltpu.roll(groups[1], 16, axis=1), top))
    first = lax.axis_index("span") == 0
    mine_ref[...] = jnp.where(first, top, bottom)
    other_ref[...] = jnp.where(first, bottom, top)


def boundary(block, wy, wx, one, two, acc):
    half = pltpu.VMEM((4, R, PAIR), BF16)
    sums = pltpu.VMEM((SUB, NX), F32)
    return pl.pallas_call(
        boundary_kernel,
        name="boundary",
        out_shape=(half, half, sums, sums),
        in_specs=[vmem_spec()] * 6,
        out_specs=(vmem_spec(),) * 4,
        scratch_shapes=[pltpu.VMEM((R, R), F32)],
        compiler_params=params(8),
    )(*in_vmem(block, wy, wx, one, two, acc))


def eliminate(work):
    row = lax.broadcasted_iota(jnp.int32, (SUB, NX), 0)

    def spread(part):
        return jnp.broadcast_to(part, (SUB, NX))

    width = SUB
    for start in range(0, S, width):
        home, base = start // SUB, start % SUB
        live = range(home, S // SUB)
        pivots = [spread(work[home][base + j : base + j + 1, :]) for j in range(width)]
        cols = [{g: spread(work[g][:, start + j : start + j + 1]) for g in live} for j in range(width)]
        heads = [[spread(cols[j][home][base + i : base + i + 1, :]) for j in range(width)] for i in range(width)]
        for i in range(width):
            scale = 1.0 / heads[i][i]
            for j in range(i + 1, width):
                ratio = heads[i][j] * scale
                pivots[j] = pivots[j] - ratio * pivots[i]
                for g in live:
                    cols[j][g] = cols[j][g] - ratio * cols[i][g]
                for k in range(j, width):
                    heads[j][k] = heads[j][k] - ratio * heads[i][k]
            for g in live:
                factor = cols[i][g] * scale
                if g == home:
                    factor = jnp.where(row > base + i, factor, 0.0)
                work[g] = work[g] - factor * pivots[i]
    return work


def modes_kernel(count, mine_ref, other_ref, edge_h_ref, edge_l_ref, last_h_ref, last_l_ref, *refs):
    parts, (out_ref, factor_ref, h_ref, l_ref, wide_ref, corner_ref, buffer, sems, in_sems) = refs[:4], refs[4:]
    loads, start = [], 0
    for k in range(2):
        width = parts[2 * k].shape[0]
        loads.append(
            [
                pltpu.make_async_copy(parts[2 * k + j], ref.at[pl.ds(start, width)], in_sems.at[2 * k + j])
                for j, ref in enumerate((h_ref, l_ref))
            ]
        )
        for load in loads[-1]:
            load.start()
        start += width
    cut = 2 * NX

    @pl.when(lax.axis_index("stream") >= 0)
    def _():
        first = lax.axis_index("span") == 0
        top = jnp.where(first, mine_ref[...], other_ref[...])
        bottom = jnp.where(first, other_ref[...], mine_ref[...])
        groups = [top, pltpu.roll(top, NX - 16, axis=1), pltpu.roll(top, NX - 32, axis=1)]
        groups += [pltpu.roll(top, NX - 64, axis=1), bottom, pltpu.roll(bottom, NX - 48, axis=1)]
        shape = (S, NX)
        row = lax.broadcasted_iota(jnp.int32, shape, 0)
        lane = lax.broadcasted_iota(jnp.int32, shape, 1)
        raw = jnp.concatenate(groups, axis=0) / count
        below = jnp.where(lane < row, raw, 0.0)
        square = jnp.concatenate([below, jnp.zeros((NX - S, NX), F32)], axis=0)
        work = jnp.where(lane <= row, raw, 0.0) + square.T[:S] + jnp.where(lane == row + NX // 2, 1.0, 0.0)
        work = jnp.concatenate(eliminate([work[g * SUB : (g + 1) * SUB] for g in range(S // SUB)]), axis=0)
        diagonal = jnp.sum(jnp.where(lane == row, work, 0.0), axis=1, keepdims=True)
        work = work * lax.rsqrt(diagonal)
        factor_ref[...] = jnp.where(lane >= row, work, 0.0)[:, :S]
        inverse = jnp.where(lane <= row, pltpu.roll(work, NX // 2, axis=1), 0.0)
        high = inverse.astype(BF16).astype(F32)
        both = jnp.concatenate([high, inverse - high], axis=0).astype(BF16)
        wide = lax.dot_general(both, lane_fold().astype(BF16), NT, preferred_element_type=F32)
        same = same_cell()
        tall_high, tall_low = (
            jnp.where(same, jnp.broadcast_to(part[:, None, :], (S, SUB, R)).reshape(R, R), 0.0)
            for part in (wide[:S], wide[S:])
        )
        half = 0.5 * tall_high
        wide_ref[...] = jnp.concatenate([m[:, :cut] for m in (tall_high, tall_low, half)], axis=1).astype(BF16)
        corner = jnp.concatenate(
            [
                jnp.concatenate([tall_high[cut:, cut:], half[cut:, cut:]], axis=1),
                jnp.concatenate([tall_low[cut:, cut:], jnp.zeros((R - cut, R - cut), F32)], axis=1),
            ],
            axis=0,
        )
        corner_ref[...] = corner.astype(BF16)

    slots = buffer.shape[0]

    group = 6

    def copy_out(place):
        q = place - group
        if q < 0:
            c, z = place // 2, place % 2 * (NZ - 1) if place < 4 else place + 2
        else:
            c, z = q // 6, q % 6 + (q < 12)
        return pltpu.make_async_copy(buffer.at[place], out_ref.at[c, :, z], sems.at[place])

    def source(place):
        if place < 4:
            return edge_h_ref[place], edge_l_ref[place]
        if place < group:
            return last_h_ref[place - 4], last_l_ref[place - 4]
        return h_ref[place - group], l_ref[place - group]

    def apply(step):
        first = step * group
        for k in range(group):
            h, l = source(first + k)
            part = jnp.dot(
                wide_ref[...], jnp.concatenate([h[:cut], h[:cut], l[:cut]], axis=0), preferred_element_type=F32
            )
            last = jnp.dot(
                corner_ref[...], jnp.concatenate([h[cut:], l[cut:]], axis=0), preferred_element_type=F32
            )
            last = part[cut:] + last[: R - cut] + last[R - cut :]
            for value, low in ((part[:cut], 0), (last, cut // SUB)):
                rows = value.shape[0] // SUB
                for half in range(2):
                    tile = value[:, half * NX : (half + 1) * NX].reshape(rows, SUB, NX)
                    buffer[first + k, low : low + rows, half * SUB : (half + 1) * SUB, :] = tile
            copy_out(first + k).start()

    @pl.when(lax.axis_index("stream") >= 0)
    def _():
        apply(0)

    for pair in loads:
        for load in pair:
            load.wait()

    @pl.when(lax.axis_index("stream") >= 0)
    def _():
        for step in range(1, 4):
            apply(step)

    for place in range(slots):
        copy_out(place).wait()


def modes_and_factor(mine, other, held, halves, count):
    return pl.pallas_call(
        functools.partial(modes_kernel, count),
        name="modes",
        out_shape=(
            pltpu.HBM((3, S, NZ, NY, NX), F32),
            jax.ShapeDtypeStruct((S, S), F32),
        ),
        in_specs=[vmem_spec()] * 6 + [any_spec()] * 4,
        out_specs=(any_spec(), vmem_spec()),
        scratch_shapes=[pltpu.VMEM((18, R, PAIR), BF16)] * 2
        + [pltpu.VMEM((R, 6 * NX), BF16), pltpu.VMEM((2 * NX, 2 * NX), BF16)]
        + [pltpu.VMEM((24, S, NY, NX), F32), pltpu.SemaphoreType.DMA((24,)), pltpu.SemaphoreType.DMA((4,))],
        compiler_params=params(32),
    )(*in_vmem(mine, other, *held), *(in_hbm(h) for h in halves))


def ring(axis, shift):
    count = lax.axis_size(axis)
    return [(i, (i + shift) % count) for i in range(count)]


def neighbours(axis, first):
    count = lax.axis_size(axis)
    pairs = [(i, (i + 1) % count) for i in range(first, count, 2)]
    return pairs + [(b, a) for a, b in pairs]


def total_over_devices(mine, other):
    swap = ring("span", 1)
    mine = mine + lax.ppermute(other, "span", swap)
    axes = ("stream", "vert")
    peers = lax.axis_size(axes)
    mine = lax.all_to_all(jnp.broadcast_to(mine, (peers,) + mine.shape), axes, 0, 0).sum(0)
    return mine, lax.ppermute(mine, "span", swap)


def per_device(velocity):
    v = velocity.reshape(3, S, ROWS, NX)
    one, two = vertical_faces(v)
    v, one, two = lax.optimization_barrier((v, one, two))
    one = lax.ppermute(one, "vert", neighbours("vert", 0))
    two = lax.ppermute(two, "vert", neighbours("vert", 1))
    xs, ys = side_faces(v)
    hy = lax.ppermute(ys, "span", ring("span", 1))
    even = lax.ppermute(xs, "stream", neighbours("stream", 0))
    odd = lax.ppermute(xs, "stream", neighbours("stream", 1))
    *head_halves, wy, wx, acc = first_component(v, hy)
    *rest_halves, wx, acc, last_high, last_low = other_components(v, hy, even, odd, wx, acc)
    *edge_halves, mine, other = boundary(v, wy, wx, one, two, acc)
    mine, other = total_over_devices(mine, other)
    devices = lax.axis_size("stream") * lax.axis_size("span") * lax.axis_size("vert")
    count = float(3 * NZ * NY * NX * devices)
    return modes_and_factor(
        mine, other, edge_halves + [last_high, last_low], head_halves + rest_halves, count
    )


def solution(mesh):
    spec = P(None, None, "vert", "span", "stream")
    return jax.shard_map(per_device, mesh=mesh, in_specs=(spec,), out_specs=(spec, P()), check_vma=False)
```

```python
import functools

import jax
import jax.numpy as jnp
from jax import lax
from jax.experimental import pallas as pl
from jax.experimental.pallas import tpu as pltpu
from jax.sharding import PartitionSpec as P

F32, BF16 = jnp.float32, jnp.bfloat16
HIGH = lax.Precision.HIGHEST
S, NZ, NY, NX = 48, 8, 16, 128
ROWS = NZ * NY
SUB = 8
R = S * SUB
PAIR = 2 * NX
MIB = 1 << 20
NT = (((1,), (1,)), ((), ()))


def any_spec():
    return pl.BlockSpec(memory_space=pl.ANY)


def vmem_spec():
    return pl.BlockSpec(memory_space=pltpu.VMEM)


def params(limit):
    return pltpu.CompilerParams(vmem_limit_bytes=limit * MIB)


def in_vmem(*arrays):
    return [pltpu.with_memory_space_constraint(a, pltpu.VMEM) for a in arrays]


def in_hbm(array):
    return pltpu.with_memory_space_constraint(array, pltpu.HBM)


def vertical_faces_kernel(v_ref, one_ref, two_ref, sems):
    odd = lax.axis_index("vert") % 2
    high = ROWS - NY
    part = S // 2
    copies = []
    for row, ref in (((1 - odd) * high, one_ref), (odd * high, two_ref)):
        rows = pl.ds(pl.multiple_of(row, NY), NY)
        for c in range(2):
            for start in range(0, S, part):
                snaps = pl.ds(start, part)
                copies.append(
                    pltpu.make_async_copy(v_ref.at[c, snaps, rows], ref.at[c, snaps], sems.at[len(copies)])
                )
    for copy in copies:
        copy.start()
    for copy in copies:
        copy.wait()


def vertical_faces(v):
    face = pltpu.VMEM((2, S, NY, NX), F32)
    return pl.pallas_call(
        vertical_faces_kernel,
        name="vertical_faces",
        out_shape=(face, face),
        in_specs=[any_spec()],
        out_specs=(vmem_spec(), vmem_spec()),
        scratch_shapes=[pltpu.SemaphoreType.DMA((8,))],
        compiler_params=params(8),
    )(in_hbm(v))


def side_faces_kernel(block_ref, x_ref, y_ref):
    lane = lax.broadcasted_iota(jnp.int32, (NY, NX), 1) // 2
    for c in (1, 2):

        def pack(z, carry, c=c):
            rows = pl.ds(pl.multiple_of(z * NY, NY), NY)
            packed = jnp.zeros((NY, NX), F32)
            for s in range(S):
                turned = pltpu.roll(block_ref[c, s, rows, :], 2 * s + 1, axis=1)
                packed = jnp.where(lane == s, turned, packed)
            x_ref[c - 1, rows, :] = packed
            return carry

        lax.fori_loop(0, NZ, pack, 0)
    first = lax.axis_index("span") == 0
    for k, c in enumerate((0, 2)):
        for s in range(S):
            high = block_ref[c, s, pl.ds(NY - 1, NZ, stride=NY), :]
            low = block_ref[c, s, pl.ds(0, NZ, stride=NY), :]
            y_ref[k, s] = jnp.where(first, high, low)


def side_faces(block):
    return pl.pallas_call(
        side_faces_kernel,
        name="side_faces",
        out_shape=(
            pltpu.VMEM((2, ROWS, NX), F32),
            pltpu.VMEM((2, S, NZ, NX), F32),
        ),
        in_specs=[vmem_spec()],
        out_specs=(vmem_spec(), vmem_spec()),
        compiler_params=params(8),
    )(*in_vmem(block))


def split_store(first, second, pair, place, h_ref, l_ref):
    for half in range(2):
        rows = slice(half * SUB, (half + 1) * SUB)
        value = jnp.concatenate([first[rows], second[rows]], axis=0)
        high = value.astype(BF16)
        low = ((value - high.astype(F32)) * 2.0).astype(BF16)
        where = (place, pl.ds(pair * 2 * SUB, 2 * SUB), pl.ds(half * NX, NX))
        h_ref[where] = high
        l_ref[where] = low


def products(h_ref, l_ref, places):
    highs, lows = [h_ref[p] for p in places], [l_ref[p] for p in places]
    left, right = jnp.concatenate(highs + highs, axis=1), jnp.concatenate(highs + lows, axis=1)
    return lax.dot_general(left, right, NT, preferred_element_type=F32)


def level(s, z):
    return slice(s * ROWS + z * NY, s * ROWS + (z + 1) * NY)


def slope_z(v_ref, c, s, z):
    return v_ref[c, level(s, z + 1), :] - v_ref[c, level(s, z - 1), :]


def slope_y(v_ref, hy_ref, c, s, z):
    row = lax.broadcasted_iota(jnp.int32, (NY, NX), 0)
    first = lax.axis_index("span") == 0
    base = s * ROWS + z * NY

    def rows(start):
        inside = min(max(start, 0), S * ROWS - SUB)
        part = v_ref[c, inside : inside + SUB, :]
        return part if inside == start else pltpu.roll(part, (inside - start) % SUB, axis=0)

    def shifted(by):
        return jnp.concatenate([rows(base + by), rows(base + SUB + by)], axis=0)

    face = hy_ref[c // 2, s, z : z + 1, :]
    up = jnp.where(row == NY - 1, jnp.where(first, face, 0.0), shifted(1))
    down = jnp.where(row == 0, jnp.where(first, 0.0, face), shifted(-1))
    return up - down


def lanes():
    return lax.broadcasted_iota(jnp.int32, (NY, NX), 1)


def inner_slope_x(v_ref, c, s, z):
    cells = v_ref[c, level(s, z), :]
    up = jnp.where(lanes() == NX - 1, 0.0, pltpu.roll(cells, NX - 1, axis=1))
    down = jnp.where(lanes() == 0, 0.0, pltpu.roll(cells, 1, axis=1))
    return up - down


def edge_slope_x(edge_ref, k, s, z):
    edge = edge_ref[k, level(0, z), :]
    if s:
        edge = pltpu.roll(edge, NX - 2 * s, axis=1)
    return jnp.where((lanes() == 0) | (lanes() == NX - 1), edge, 0.0)


def send_out(places, scratch, refs, sems):
    for i, (a, b) in enumerate(zip(scratch, refs)):
        for p in places:
            pltpu.make_async_copy(a.at[p], b.at[p], sems.at[i]).start()


def wait_out(scratch, refs, sems):
    for i, (a, b) in enumerate(zip(scratch, refs)):
        pltpu.make_async_copy(a, b, sems.at[i]).wait()


def first_kernel(v_ref, hy_ref, h_out, l_out, part_ref, wx_ref, acc_ref, h_ref, l_ref, sems):
    def vorticity(z):
        for s in range(0, S, 2):
            pair = (0.5 * (slope_y(v_ref, hy_ref, 2, t, z) - slope_z(v_ref, 1, t, z)) for t in (s, s + 1))
            split_store(*pair, s // 2, z - 1, h_ref, l_ref)
        send_out([z - 1], (h_ref, l_ref), (h_out, l_out), sems)

    def slopes(z):
        for s in range(S):
            wx_ref[level(s, z), :] = inner_slope_x(v_ref, 2, s, z)

    vorticity(1)
    slopes(0)
    slopes(1)
    vorticity(2)
    slopes(2)
    acc_ref[...] = products(h_ref, l_ref, [0])
    for z in range(3, NZ - 1):
        vorticity(z)
        slopes(z)
        acc_ref[...] += products(h_ref, l_ref, [z - 2])
    for k in range(2):
        for s in range(S):
            part_ref[k, s] = slope_y(v_ref, hy_ref, 2, s, k * (NZ - 1))
    slopes(NZ - 1)
    acc_ref[...] += products(h_ref, l_ref, [NZ - 3])

    @pl.when(lax.axis_index("span") >= 0)
    def _():
        wait_out((h_ref, l_ref), (h_out, l_out), sems)

def first_component(block, hy):
    block = block.reshape(3, S * ROWS, NX)
    half = pltpu.HBM((6, R, PAIR), BF16)
    return pl.pallas_call(
        first_kernel,
        name="first_component",
        out_shape=(
            half,
            half,
            pltpu.VMEM((2, S, NY, NX), F32),
            pltpu.VMEM((S * ROWS, NX), F32),
            pltpu.VMEM((R, R), F32),
        ),
        in_specs=[vmem_spec()] * 2,
        out_specs=(any_spec(), any_spec(), vmem_spec(), vmem_spec(), vmem_spec()),
        scratch_shapes=[pltpu.VMEM((6, R, PAIR), BF16)] * 2 + [pltpu.SemaphoreType.DMA((2,))],
        compiler_params=params(8),
        cost_estimate=pl.CostEstimate(flops=4 * R * R * 6 * PAIR, bytes_accessed=6 * MIB, transcendentals=0),
    )(*in_vmem(block, hy))


def rest_kernel(
    v_ref, hy_ref, even_ref, odd_ref, wx_ref, old_ref, h_out, l_out, part_ref, acc_ref, h_last, l_last,
    edge_ref, h_ref, l_ref, sems
):
    lane = lanes()
    stream = lax.axis_index("stream")
    even = stream % 2 == 0
    for c in range(2):
        for z in range(NZ):
            rows = pl.ds(z * NY, NY)
            one, two = even_ref[c, rows, :], odd_ref[c, rows, :]
            left, right = jnp.where(even, two, one), jnp.where(even, one, two)
            before = jnp.where(stream > 0, left, 0.0)
            behind = jnp.where(stream < lax.axis_size("stream") - 1, right, 0.0)
            edge_ref[c, rows, :] = jnp.where(lane % 2 == 0, -before, pltpu.roll(behind, NX - 2, axis=1))

    def slope_wx(s, z):
        return wx_ref[level(s, z), :] + edge_slope_x(edge_ref, 1, s, z)

    def second(z):
        for s in range(0, S, 2):
            pair = (0.5 * (slope_z(v_ref, 0, t, z) - slope_wx(t, z)) for t in (s, s + 1))
            split_store(*pair, s // 2, z - 1, h_ref, l_ref)
        send_out([z - 1], (h_ref, l_ref), (h_out, l_out), sems)

    def third(z):
        for s in range(0, S, 2):
            pair = (
                0.5
                * (inner_slope_x(v_ref, 1, t, z) + edge_slope_x(edge_ref, 0, t, z) - slope_y(v_ref, hy_ref, 0, t, z))
                for t in (s, s + 1)
            )
            if z < NZ - 2:
                split_store(*pair, s // 2, z + 6, h_ref, l_ref)
            else:
                split_store(*pair, s // 2, z - NZ + 2, h_last, l_last)
        if z < NZ - 2:
            send_out([z + 6], (h_ref, l_ref), (h_out, l_out), sems)

    third(0)
    second(1)
    third(1)
    acc_ref[...] = old_ref[...] + products(h_ref, l_ref, [6])
    for z in range(2, NZ - 1):
        second(z)
        third(z)
        acc_ref[...] += products(h_ref, l_ref, [z - 2, z + 5])
    third(NZ - 1)
    acc_ref[...] += products(h_ref, l_ref, [NZ - 3])
    for k in range(2):
        for s in range(S):
            part_ref[k, s] = slope_wx(s, k * (NZ - 1))
    acc_ref[...] += products(h_last, l_last, range(2))

    @pl.when(stream >= 0)
    def _():
        wait_out((h_ref, l_ref), (h_out, l_out), sems)


def other_components(block, hy, even, odd, wx, acc):
    block = block.reshape(3, S * ROWS, NX)
    half, last = pltpu.HBM((12, R, PAIR), BF16), pltpu.VMEM((2, R, PAIR), BF16)
    return pl.pallas_call(
        rest_kernel,
        name="other_components",
        out_shape=(half, half, pltpu.VMEM((2, S, NY, NX), F32), pltpu.VMEM((R, R), F32), last, last),
        in_specs=[vmem_spec()] * 6,
        out_specs=(any_spec(), any_spec()) + (vmem_spec(),) * 4,
        scratch_shapes=[pltpu.VMEM((2, ROWS, NX), F32)]
        + [pltpu.VMEM((12, R, PAIR), BF16)] * 2
        + [pltpu.SemaphoreType.DMA((2,))],
        compiler_params=params(12),
        cost_estimate=pl.CostEstimate(flops=4 * R * R * 14 * PAIR, bytes_accessed=12 * MIB, transcendentals=0),
    )(*in_vmem(block, hy, even, odd, wx, acc))


def lane_fold():
    shape = (R, NX)
    same = lax.broadcasted_iota(jnp.int32, shape, 0) // SUB == lax.broadcasted_iota(jnp.int32, shape, 1)
    return jnp.where(same, 1.0, 0.0)


def same_cell():
    return lax.broadcasted_iota(jnp.int32, (R, R), 0) % SUB == lax.broadcasted_iota(jnp.int32, (R, R), 1) % SUB


def edge_level(which, v_ref, wy_ref, wx_ref, face_ref, acc_ref, h_ref, l_ref, sum_ref):
    vert = lax.axis_index("vert")

    def vorticity(k):
        inside = vert < lax.axis_size("vert") - 1 if k else vert > 0

        def dz(c, s):
            face = jnp.where(inside, face_ref[c, s], 0.0)
            if k:
                return face - v_ref[c, s, pl.ds((NZ - 2) * NY, NY), :]
            return v_ref[c, s, pl.ds(NY, NY), :] - face

        for s in range(0, S, 2):
            first = (0.5 * (wy_ref[k, t] - dz(1, t)) for t in (s, s + 1))
            split_store(*first, s // 2, 0, h_ref, l_ref)
        for s in range(0, S, 2):
            second = (0.5 * (dz(0, t) - wx_ref[k, t]) for t in (s, s + 1))
            split_store(*second, s // 2, 1, h_ref, l_ref)
        sum_ref[...] = acc_ref[...] + products(h_ref, l_ref, range(2))

    @pl.when(vert % 2 == which)
    def _():
        vorticity(1)

    @pl.when(vert % 2 == 1 - which)
    def _():
        vorticity(0)


def last_edge_kernel(v_ref, wy_ref, wx_ref, face_ref, acc_ref, h_ref, l_ref, mine_ref, other_ref, sum_ref):
    edge_level(1, v_ref, wy_ref, wx_ref, face_ref, acc_ref, h_ref, l_ref, sum_ref)
    total = sum_ref[...]
    total = jnp.where(same_cell(), total, 0.0).reshape(S, SUB, R).sum(1)
    total = lax.dot_general(
        total, lane_fold(), (((1,), (0,)), ((), ())), precision=HIGH, preferred_element_type=F32
    )
    square = jnp.concatenate([total, jnp.zeros((NX - S, NX), F32)], axis=0)
    total = 0.5 * (total + square.T[:S])
    lane = lax.broadcasted_iota(jnp.int32, (SUB, NX), 1)
    groups = [total[g * SUB : (g + 1) * SUB] for g in range(S // SUB)]
    bottom = jnp.where(lane < 48, groups[4], pltpu.roll(groups[5], 48, axis=1))
    top = jnp.where(lane < 64, pltpu.roll(groups[2], 32, axis=1), pltpu.roll(groups[3], 64, axis=1))
    top = jnp.where(lane < 16, groups[0], jnp.where(lane < 32, pltpu.roll(groups[1], 16, axis=1), top))
    first = lax.axis_index("span") == 0
    mine_ref[...] = jnp.where(first, top, bottom)
    other_ref[...] = jnp.where(first, bottom, top)


def edge(which, block, wy, wx, face, acc):
    half = pltpu.VMEM((2, R, PAIR), BF16)
    sums = pltpu.VMEM((SUB, NX), F32)
    square = pltpu.VMEM((R, R), F32)
    return pl.pallas_call(
        last_edge_kernel if which else functools.partial(edge_level, 0),
        name="last_edge" if which else "first_edge",
        out_shape=(half, half, sums, sums) if which else (half, half, square),
        in_specs=[vmem_spec()] * 5,
        out_specs=(vmem_spec(),) * (4 if which else 3),
        scratch_shapes=[square] if which else [],
        compiler_params=params(8),
    )(*in_vmem(block, wy, wx, face, acc))


def eliminate(work):
    row = lax.broadcasted_iota(jnp.int32, (SUB, NX), 0)

    def spread(part):
        return jnp.broadcast_to(part, (SUB, NX))

    width = SUB
    for start in range(0, S, width):
        home, base = start // SUB, start % SUB
        live = range(home, S // SUB)
        pivots = [spread(work[home][base + j : base + j + 1, :]) for j in range(width)]
        cols = [{g: spread(work[g][:, start + j : start + j + 1]) for g in live} for j in range(width)]
        heads = [[spread(cols[j][home][base + i : base + i + 1, :]) for j in range(width)] for i in range(width)]
        for i in range(width):
            scale = 1.0 / heads[i][i]
            for j in range(i + 1, width):
                ratio = heads[i][j] * scale
                pivots[j] = pivots[j] - ratio * pivots[i]
                for g in live:
                    cols[j][g] = cols[j][g] - ratio * cols[i][g]
                for k in range(j, width):
                    heads[j][k] = heads[j][k] - ratio * heads[i][k]
            for g in live:
                factor = cols[i][g] * scale
                if g == home:
                    factor = jnp.where(row > base + i, factor, 0.0)
                work[g] = work[g] - factor * pivots[i]
    return work


def modes_kernel(count, mine_ref, other_ref, *refs):
    kept, refs = refs[:6], refs[6:]
    parts, (out_ref, factor_ref, h_ref, l_ref, wide_ref, corner_ref, buffer, sems, in_sems) = refs[:4], refs[4:]
    loads, start = [], 0
    for k in range(2):
        width = parts[2 * k].shape[0]
        loads.append(
            [
                pltpu.make_async_copy(parts[2 * k + j], ref.at[pl.ds(start, width)], in_sems.at[2 * k + j])
                for j, ref in enumerate((h_ref, l_ref))
            ]
        )
        for load in loads[-1]:
            load.start()
        start += width
    cut = 2 * NX

    @pl.when(lax.axis_index("stream") >= 0)
    def _():
        first = lax.axis_index("span") == 0
        top = jnp.where(first, mine_ref[...], other_ref[...])
        bottom = jnp.where(first, other_ref[...], mine_ref[...])
        groups = [top, pltpu.roll(top, NX - 16, axis=1), pltpu.roll(top, NX - 32, axis=1)]
        groups += [pltpu.roll(top, NX - 64, axis=1), bottom, pltpu.roll(bottom, NX - 48, axis=1)]
        shape = (S, NX)
        row = lax.broadcasted_iota(jnp.int32, shape, 0)
        lane = lax.broadcasted_iota(jnp.int32, shape, 1)
        raw = jnp.concatenate(groups, axis=0) / count
        below = jnp.where(lane < row, raw, 0.0)
        square = jnp.concatenate([below, jnp.zeros((NX - S, NX), F32)], axis=0)
        work = jnp.where(lane <= row, raw, 0.0) + square.T[:S] + jnp.where(lane == row + NX // 2, 1.0, 0.0)
        work = jnp.concatenate(eliminate([work[g * SUB : (g + 1) * SUB] for g in range(S // SUB)]), axis=0)
        diagonal = jnp.sum(jnp.where(lane == row, work, 0.0), axis=1, keepdims=True)
        work = work * lax.rsqrt(diagonal)
        factor_ref[...] = jnp.where(lane >= row, work, 0.0)[:, :S]
        inverse = jnp.where(lane <= row, pltpu.roll(work, NX // 2, axis=1), 0.0)
        high = inverse.astype(BF16).astype(F32)
        both = jnp.concatenate([high, inverse - high], axis=0).astype(BF16)
        wide = lax.dot_general(both, lane_fold().astype(BF16), NT, preferred_element_type=F32)
        same = same_cell()
        tall_high, tall_low = (
            jnp.where(same, jnp.broadcast_to(part[:, None, :], (S, SUB, R)).reshape(R, R), 0.0)
            for part in (wide[:S], wide[S:])
        )
        half = 0.5 * tall_high
        wide_ref[...] = jnp.concatenate([m[:, :cut] for m in (tall_high, tall_low, half)], axis=1).astype(BF16)
        corner = jnp.concatenate(
            [
                jnp.concatenate([tall_high[cut:, cut:], half[cut:, cut:]], axis=1),
                jnp.concatenate([tall_low[cut:, cut:], jnp.zeros((R - cut, R - cut), F32)], axis=1),
            ],
            axis=0,
        )
        corner_ref[...] = corner.astype(BF16)

    slots = buffer.shape[0]

    group = 6

    def copy_out(place):
        q = place - group
        if q < 0:
            odd = lax.axis_index("vert") % 2
            c, z = (place % 2, (1 - odd, odd)[place // 2] * (NZ - 1)) if place < 4 else (2, place + 2)
        else:
            c, z = q // 6, q % 6 + (q < 12)
        return pltpu.make_async_copy(buffer.at[place], out_ref.at[c, :, z], sems.at[place])

    def source(place):
        if place < group:
            return tuple(ref[place % 2] for ref in kept[place // 2 * 2 : place // 2 * 2 + 2])
        return h_ref[place - group], l_ref[place - group]

    def apply(step):
        first = step * group
        for k in range(group):
            h, l = source(first + k)
            part = jnp.dot(
                wide_ref[...], jnp.concatenate([h[:cut], h[:cut], l[:cut]], axis=0), preferred_element_type=F32
            )
            last = jnp.dot(
                corner_ref[...], jnp.concatenate([h[cut:], l[cut:]], axis=0), preferred_element_type=F32
            )
            last = part[cut:] + last[: R - cut] + last[R - cut :]
            for value, low in ((part[:cut], 0), (last, cut // SUB)):
                rows = value.shape[0] // SUB
                for half in range(2):
                    tile = value[:, half * NX : (half + 1) * NX].reshape(rows, SUB, NX)
                    buffer[first + k, low : low + rows, half * SUB : (half + 1) * SUB, :] = tile
            copy_out(first + k).start()

    @pl.when(lax.axis_index("stream") >= 0)
    def _():
        apply(0)

    for pair in loads:
        for load in pair:
            load.wait()

    @pl.when(lax.axis_index("stream") >= 0)
    def _():
        for step in range(1, 4):
            apply(step)

    for place in range(slots):
        copy_out(place).wait()


def modes_and_factor(mine, other, held, halves, count):
    return pl.pallas_call(
        functools.partial(modes_kernel, count),
        name="modes",
        out_shape=(
            pltpu.HBM((3, S, NZ, NY, NX), F32),
            jax.ShapeDtypeStruct((S, S), F32),
        ),
        in_specs=[vmem_spec()] * 8 + [any_spec()] * 4,
        out_specs=(any_spec(), vmem_spec()),
        scratch_shapes=[pltpu.VMEM((18, R, PAIR), BF16)] * 2
        + [pltpu.VMEM((R, 6 * NX), BF16), pltpu.VMEM((2 * NX, 2 * NX), BF16)]
        + [pltpu.VMEM((24, S, NY, NX), F32), pltpu.SemaphoreType.DMA((24,)), pltpu.SemaphoreType.DMA((4,))],
        compiler_params=params(32),
    )(*in_vmem(mine, other, *held), *(in_hbm(h) for h in halves))


def ring(axis, shift):
    count = lax.axis_size(axis)
    return [(i, (i + shift) % count) for i in range(count)]


def neighbours(axis, first):
    count = lax.axis_size(axis)
    pairs = [(i, (i + 1) % count) for i in range(first, count, 2)]
    return pairs + [(b, a) for a, b in pairs]


def total_over_devices(mine, other):
    swap = ring("span", 1)
    mine = mine + lax.ppermute(other, "span", swap)
    axes = ("stream", "vert")
    peers = lax.axis_size(axes)
    mine = lax.all_to_all(jnp.broadcast_to(mine, (peers,) + mine.shape), axes, 0, 0).sum(0)
    return mine, lax.ppermute(mine, "span", swap)


def per_device(velocity):
    v = velocity.reshape(3, S, ROWS, NX)
    one, two = vertical_faces(v)
    v, one, two = lax.optimization_barrier((v, one, two))
    one = lax.ppermute(one, "vert", neighbours("vert", 0))
    two = lax.ppermute(two, "vert", neighbours("vert", 1))
    xs, ys = side_faces(v)
    hy = lax.ppermute(ys, "span", ring("span", 1))
    even = lax.ppermute(xs, "stream", neighbours("stream", 0))
    odd = lax.ppermute(xs, "stream", neighbours("stream", 1))
    *head_halves, wy, wx, acc = first_component(v, hy)
    *rest_halves, wx, acc, last_high, last_low = other_components(v, hy, even, odd, wx, acc)
    *near_halves, acc = edge(0, v, wy, wx, one, acc)
    *far_halves, mine, other = edge(1, v, wy, wx, two, acc)
    mine, other = total_over_devices(mine, other)
    devices = lax.axis_size("stream") * lax.axis_size("span") * lax.axis_size("vert")
    count = float(3 * NZ * NY * NX * devices)
    return modes_and_factor(
        mine, other, near_halves + far_halves + [last_high, last_low], head_halves + rest_halves, count
    )


def solution(mesh):
    spec = P(None, None, "vert", "span", "stream")
    return jax.shard_map(per_device, mesh=mesh, in_specs=(spec,), out_specs=(spec, P()), check_vma=False)
```
